128 devices in a mesh: grp: 4 (over z), tm: 32 (over y, x, core).
Axes of the slice: x: 4, y: 4, z: 4, core: 2. Of those that a mesh axis runs over, the one named last changes fastest.
Arguments:
- frames: bfloat16 [4, 128, 24, 24, 2048], P('grp', 'tm'), may hold values from -6 to 6
- sample_counts: int32 [4, 128], P('grp', 'tm'), may hold values from 0 to 3, as said below
- dest_groups: int32 [4, 128], P('grp', 'tm'), may hold values from 0 to 3, as said below
- episode_ends: int32 [4, 128], P('grp', 'tm'), may hold values 0 or 1
- valid_steps: int32 [4, 128], P('grp', 'tm'), may hold values 0 or 1
- rewards: float32 [4, 128], P('grp', 'tm'), may hold values from -1.25 to 1.25
- ratios: float32 [4, 128], P('grp', 'tm'), may hold values from 0.5 to 1.04
- stored_values: float32 [4, 128, 128], P('grp', 'tm'), may hold values from -6 to 6
- stem_weight: bfloat16 [2048, 256], replicated, may hold values from -0.125 to 0.125
- conv_first: bfloat16 [2, 9, 256, 256], replicated, may hold values from -0.125 to 0.125
- conv_second: bfloat16 [2, 9, 256, 256], replicated, may hold values from -0.125 to 0.125
- value_weight: bfloat16 [256, 128], replicated, may hold values from -0.375 to 0.375
- discounts: float32 [128], replicated, may hold values from 0.97 to 1
- lambdas: float32 [128], replicated, may hold values from 0.95 to 1
Outputs:
- latents: bfloat16 [4, 128, 24, 24, 256], P('grp', 'tm')
- values: float32 [4, 128, 128], P('grp', 'tm')
- targets: float32 [4, 128, 128], P('grp', 'tm')
- group_load: int32 [4, 32], P('grp', 'tm')
The draws below stay inside these ranges and needn't reach their ends.
Inputs may be any that keep to these rules, and one draw needn't show every extreme that they name: `sample_counts`: in every time shard, one of the 4 devices holding it has all 4 of its blocks sampled. `dest_groups`: read only for sampled blocks. At most 1 sampled blocks of one device name the same group, and at most 2 sampled blocks of one time shard (over all groups) name the same group; both bounds are reached in every draw.
All inputs are finite; a program needn't handle non-finite values. No bound on the sum of `episode_ends` or of `valid_steps` on one device may be relied on, other than what follows from the above.
Results may differ from the reference program's by a relative error of at most 0.014.
Values may be sent and summed in bfloat16 or wider, within the bound.
No kernel may reach another device: no remote copies, remote signals or barrier semaphores. Data moves between devices by JAX's collectives and lax.ppermute only.
A program may use at most 128 MiB of HBM per device.

```python
import jax
import jax.numpy as jnp
from jax import lax

SIDE = 24
PDIM = 2048
C = 256
VCH = 128
RES_BLOCKS = 2
TIME_DEV = 4
MEMORY_BATCHES = 4
SHARDS = 32
HORIZON_LENGTH = 128


def routing_plan(key):
    hot_key, pick_key, perm_key = jax.random.split(key, 3)
    per_pair = TIME_DEV // MEMORY_BATCHES
    hot_group = jax.random.randint(hot_key, (SHARDS,), 0, MEMORY_BATCHES)
    picked = jax.random.randint(pick_key, (SHARDS, MEMORY_BATCHES), 0, MEMORY_BATCHES - 1)
    sender = picked + (picked >= hot_group[:, None]).astype(jnp.int32)
    group_ids = jnp.arange(MEMORY_BATCHES, dtype=jnp.int32)
    sent_pairs = (group_ids[None, :, None] == hot_group[:, None, None]).astype(jnp.int32) + (sender[:, None, :] == group_ids[None, :, None]).astype(jnp.int32)
    slot_dest = jnp.arange(TIME_DEV, dtype=jnp.int32) // per_pair
    live_slot = sent_pairs[:, :, slot_dest] > 0
    perm_keys = jax.random.split(perm_key, SHARDS * MEMORY_BATCHES)
    shuffles = jax.vmap(lambda one_key: jax.random.permutation(one_key, TIME_DEV))(perm_keys)
    shuffles = shuffles.reshape(SHARDS, MEMORY_BATCHES, TIME_DEV)
    inverse = jnp.argsort(shuffles, axis=-1)
    block_live = jnp.take_along_axis(live_slot, inverse, axis=-1)
    block_dest = slot_dest[inverse]
    block_live = jnp.transpose(block_live, (1, 0, 2)).reshape(MEMORY_BATCHES, SHARDS * TIME_DEV)
    block_dest = jnp.transpose(block_dest, (1, 0, 2)).reshape(MEMORY_BATCHES, SHARDS * TIME_DEV)
    return (block_live, block_dest)


def horizon_split(key, fraction):
    return jax.random.uniform(key, (VCH,)) < fraction


def draw_sample_counts(key, part):
    block_live, block_dest = routing_plan(key)
    key = jax.random.fold_in(key, 5)
    drawn = jax.random.randint(key, (MEMORY_BATCHES, HORIZON_LENGTH), 1, 4)
    return jnp.where(block_live, drawn, 0).astype(jnp.int32)


def draw_dest_groups(key, part):
    block_live, block_dest = routing_plan(key)
    key = jax.random.fold_in(key, 7)
    filler = jax.random.randint(key, (MEMORY_BATCHES, HORIZON_LENGTH), 0, MEMORY_BATCHES)
    return jnp.where(block_live, block_dest, filler).astype(jnp.int32)


def draw_discounts(key, part):
    slow_heads = horizon_split(key, 0.5)
    key = jax.random.fold_in(key, 11)
    spread = jax.random.uniform(key, (VCH,))
    slow_gap = 0.05 / HORIZON_LENGTH * jnp.exp(spread * jnp.log(5.0))
    fast_gap = 0.01 * jnp.exp(spread * jnp.log(3.0))
    return (1.0 - jnp.where(slow_heads, slow_gap, fast_gap)).astype(jnp.float32)


def draw_lambdas(key, part):
    slow_heads = horizon_split(key, 0.5)
    key = jax.random.fold_in(key, 13)
    spread = jax.random.uniform(key, (VCH,))
    slow_value = 1.0 - 0.05 / HORIZON_LENGTH * jnp.exp(spread * jnp.log(5.0))
    fast_value = 0.95 + 0.03 * spread
    return jnp.where(slow_heads, slow_value, fast_value).astype(jnp.float32)


def draw_ratios(key, part):
    key = jax.random.fold_in(key, 17)
    master_seed, rollout_segment_seed, encoder_layer_seed = jax.random.split(key, 3)
    reference_estimate = jnp.exp(0.006 * jnp.clip(jax.random.normal(master_seed, (MEMORY_BATCHES, HORIZON_LENGTH)), -5.0, 5.0))
    rollout_segments = jax.random.uniform(rollout_segment_seed, (MEMORY_BATCHES, HORIZON_LENGTH)) < 1.5 / HORIZON_LENGTH
    encoder_layer_total = jax.random.uniform(encoder_layer_seed, (MEMORY_BATCHES, HORIZON_LENGTH), minval=0.5, maxval=0.8)
    return jnp.where(rollout_segments, encoder_layer_total, reference_estimate).astype(jnp.float32)


def plant(entries, stream_key, low, top_value):
    longest = entries.shape.index(max(entries.shape))
    spots = []
    for shift in (0, 1):
        where = [jax.random.randint(jax.random.fold_in(stream_key, axis), (), 0, length) for axis, length in enumerate(entries.shape)]
        where[longest] = (where[longest] + shift) % entries.shape[longest]
        spots.append(tuple(where))
    return entries.at[spots[0]].set(low).at[spots[1]].set(top_value)


def block_scale(own_key, extent, cuts, least, largest):
    factor_of, own = 1.0, jax.random.fold_in(own_key, 6)
    for axis_at, shards_of in cuts:
        draws = jnp.exp(jax.random.uniform(jax.random.fold_in(own, axis_at), (shards_of,), jnp.float32, least / len(cuts), largest / len(cuts)))
        factor_of = factor_of * jnp.repeat(draws, extent[axis_at] // shards_of).reshape([-1 if axis == axis_at else 1 for axis in range(len(extent))])
    return factor_of


def noise(stream_key, dims, scale, limit, shards=(), kind=jnp.bfloat16):
    level = block_scale(stream_key, dims, shards, -0.22, 0.18) if shards else 1.0
    array = jax.random.normal(stream_key, dims, jnp.float32) * scale * level
    return jnp.minimum(jnp.maximum(array, -limit), limit).astype(kind)


def setup_inputs(seed: int = 0) -> dict:
    streams_of = jax.random.split(jax.random.key(seed), 15)
    frames = noise(streams_of[0], (MEMORY_BATCHES, HORIZON_LENGTH, SIDE, SIDE, PDIM), 1.0, 6.0, ((0, 4), (1, 32)))
    sample_counts = draw_sample_counts(jax.random.fold_in(streams_of[14], 71), 0)
    dest_groups = draw_dest_groups(jax.random.fold_in(streams_of[14], 71), 0)
    episode_ends = plant((jax.random.randint(streams_of[3], (MEMORY_BATCHES, HORIZON_LENGTH), 0, 2 * HORIZON_LENGTH) < 1).astype(jnp.int32), jax.random.fold_in(streams_of[3], 1), 0, 1)
    valid_steps = plant((jax.random.randint(streams_of[4], (MEMORY_BATCHES, HORIZON_LENGTH), 0, 8) < 7).astype(jnp.int32), jax.random.fold_in(streams_of[4], 1), 0, 1)
    rewards = noise(streams_of[5], (MEMORY_BATCHES, HORIZON_LENGTH), (HORIZON_LENGTH ** -0.5), 1.25, ((0, 4), (1, 32)), jnp.float32)
    ratios = draw_ratios(jax.random.fold_in(streams_of[14], 71), 0)
    stored_values = noise(streams_of[7], (MEMORY_BATCHES, HORIZON_LENGTH, VCH), 1.0, 6.0, ((0, 4), (1, 32)), jnp.float32)
    stem_weight = noise(streams_of[8], (PDIM, C), PDIM ** -0.5, 0.125)
    conv_first = noise(streams_of[9], (RES_BLOCKS, 9, C, C), (9 * C) ** -0.5, 0.125)
    conv_second = noise(streams_of[10], (RES_BLOCKS, 9, C, C), (9 * C) ** -0.5, 0.125)
    value_weight = noise(streams_of[11], (C, VCH), C ** -0.5, 0.375)
    discounts = draw_discounts(jax.random.fold_in(streams_of[14], 71), 0)
    lambdas = draw_lambdas(jax.random.fold_in(streams_of[14], 71), 0)
    return {"frames": frames, "sample_counts": sample_counts, "dest_groups": dest_groups, "episode_ends": episode_ends, "valid_steps": valid_steps, "rewards": rewards, "ratios": ratios, "stored_values": stored_values, "stem_weight": stem_weight, "conv_first": conv_first, "conv_second": conv_second, "value_weight": value_weight, "discounts": discounts, "lambdas": lambdas}


def conv_tap(source, weight):
    count_rows, grid_side, _, channels = source.shape
    padded = jnp.pad(source, ((0, 0), (1, 1), (1, 1), (0, 0)))
    accumulated = jnp.zeros((count_rows * grid_side * grid_side, weight.shape[2]), jnp.float32)
    for tap_index in range(9):
        tap_row = tap_index // 3
        tap_col = tap_index % 3
        window = padded[:, tap_row:tap_row + grid_side, tap_col:tap_col + grid_side, :]
        window = window.reshape(count_rows * grid_side * grid_side, channels)
        accumulated = accumulated + jnp.dot(window, weight[tap_index], preferred_element_type=jnp.float32)
    return accumulated.reshape(count_rows, grid_side, grid_side, weight.shape[2])

def stem_layer(blocks, stem_weight):
    count_rows, grid_side, _, patch_values = blocks.shape
    hidden = jnp.dot(blocks.reshape(-1, patch_values), stem_weight, preferred_element_type=jnp.float32)
    hidden = jax.nn.relu(hidden).astype(jnp.bfloat16)
    return hidden.reshape(count_rows, grid_side, grid_side, stem_weight.shape[1])

def residual_tower(hidden, conv_first, conv_second):
    for layer_index in range(conv_first.shape[0]):
        widened = hidden.astype(jnp.float32)
        normed = widened * lax.rsqrt(lax.optimization_barrier(jnp.mean(widened * widened, axis=-1, keepdims=True)) + 1e-05)
        activated = jax.nn.relu(normed).astype(jnp.bfloat16)
        middle = jax.nn.relu(conv_tap(activated, conv_first[layer_index])).astype(jnp.bfloat16)
        hidden = (widened + conv_tap(middle, conv_second[layer_index])).astype(jnp.bfloat16)
    return hidden

def reference(frames, sample_counts, dest_groups, episode_ends, valid_steps, rewards, ratios, stored_values, stem_weight, conv_first, conv_second, value_weight, discounts, lambdas):
    block_total = MEMORY_BATCHES * HORIZON_LENGTH
    flat_frames = frames.reshape(block_total, SIDE, SIDE, PDIM)
    sampled = sample_counts.reshape(block_total) > 0
    positions = jnp.arange(block_total, dtype=jnp.int32)
    order_key = jnp.where(sampled, positions, positions + block_total)
    slot_order = jnp.argsort(order_key)[:block_total // 2].astype(jnp.int32)

    def encode_one(block_index):
        single = lax.dynamic_slice_in_dim(flat_frames, block_index.astype(jnp.int32), 1, 0)
        return residual_tower(stem_layer(single, stem_weight), conv_first, conv_second)[0]
    encoded = lax.map(encode_one, slot_order)
    latents = jnp.zeros((block_total, SIDE, SIDE, C), jnp.bfloat16).at[slot_order].set(encoded)
    latents = jnp.where(sampled[:, None, None, None], latents, jnp.zeros_like(latents))
    pooled = lax.optimization_barrier(jnp.mean(latents.astype(jnp.float32), axis=(1, 2)))
    fresh_values = jnp.dot(pooled, value_weight.astype(jnp.float32), precision=lax.Precision.HIGHEST)
    values = jnp.where(sampled[:, None], fresh_values, stored_values.reshape(block_total, VCH))
    values = values.reshape(MEMORY_BATCHES, HORIZON_LENGTH, VCH)
    continuing = 1.0 - episode_ends.astype(jnp.float32)
    trace_cut = jnp.minimum(1.0, ratios)
    next_values = jnp.concatenate([values[:, 1:], jnp.zeros((MEMORY_BATCHES, 1, VCH), jnp.float32)], axis=1)
    add_terms = rewards[..., None] + discounts * continuing[..., None] * (1.0 - lambdas * trace_cut[..., None]) * next_values
    mul_terms = discounts * lambdas * trace_cut[..., None] * continuing[..., None]

    def back_step(carry, inputs):
        add_term, mul_term = inputs
        updated = add_term + mul_term * carry
        return (updated, updated)
    _, returns = lax.scan(back_step, jnp.zeros((MEMORY_BATCHES, VCH), jnp.float32), (jnp.transpose(add_terms, (1, 0, 2)), jnp.transpose(mul_terms, (1, 0, 2))), reverse=True)
    targets = valid_steps.astype(jnp.float32)[..., None] * jnp.transpose(returns, (1, 0, 2))
    routed_hits = (dest_groups[..., None] == jnp.arange(MEMORY_BATCHES, dtype=jnp.int32)) & (sample_counts > 0)[..., None]
    weighted = jnp.where(routed_hits, sample_counts[..., None], 0).reshape(MEMORY_BATCHES, SHARDS, TIME_DEV, MEMORY_BATCHES)
    group_load = jnp.transpose(lax.optimization_barrier(jnp.sum(weighted, axis=(0, 2)))).astype(jnp.int32)
    return (latents.reshape(MEMORY_BATCHES, HORIZON_LENGTH, SIDE, SIDE, C), values, targets, group_load)
```

```python
import jax
import jax.numpy as jnp
from jax import lax
from jax.experimental import pallas as pl
from jax.experimental.pallas import tpu as pltpu
from jax.sharding import PartitionSpec as P

BF = jnp.bfloat16
F32 = jnp.float32


def conv(x, w):
    return lax.conv_general_dilated(
        x,
        w.reshape(3, 3, w.shape[1], w.shape[2]),
        (1, 1),
        "SAME",
        dimension_numbers=("NHWC", "HWIO", "NHWC"),
        preferred_element_type=F32,
    )


def encode(blocks, counts, stem_weight, conv_first, conv_second):
    steps, side, _, pdim = blocks.shape
    channels = stem_weight.shape[1]
    hidden = jnp.dot(blocks.reshape(-1, pdim), stem_weight, preferred_element_type=F32)
    hidden = jax.nn.relu(hidden).astype(BF).reshape(steps, side, side, channels)
    for layer in range(conv_first.shape[0]):
        wide = hidden.astype(F32)
        normed = wide * lax.rsqrt(jnp.mean(wide * wide, axis=-1, keepdims=True) + 1e-05)
        activated = jax.nn.relu(normed).astype(BF)
        middle = jax.nn.relu(conv(activated, conv_first[layer])).astype(BF)
        hidden = (wide + conv(middle, conv_second[layer])).astype(BF)
    latents = jnp.where((counts > 0)[:, None, None, None], hidden, jnp.zeros_like(hidden))
    pooled = jnp.mean(latents.astype(F32), axis=(1, 2))
    return latents, pooled


def head_kernel(
    steps,
    counts_ref,
    ends_ref,
    rewards_ref,
    ratios_ref,
    pooled_ref,
    stored_ref,
    head_ref,
    discounts_ref,
    lambdas_ref,
    values_ref,
    send_ref,
    chain_ref,
):
    fresh = jnp.dot(
        pooled_ref[...],
        head_ref[...].astype(F32),
        precision=lax.Precision.HIGHEST,
        preferred_element_type=F32,
    )
    discount = discounts_ref[...]
    trace = lambdas_ref[...]
    rows = []
    for t in range(steps):
        live = jnp.full((1, fresh.shape[1]), counts_ref[0, t], jnp.int32) > 0
        rows.append(jnp.where(live, fresh[t : t + 1], stored_ref[t : t + 1]))
        values_ref[t : t + 1] = rows[t]
    add = jnp.zeros_like(discount)
    mul = jnp.ones_like(discount)
    last = jnp.zeros_like(discount)
    for t in range(steps - 1, -1, -1):
        going = 1.0 - ends_ref[0, t].astype(F32)
        cut = jnp.minimum(1.0, ratios_ref[0, t])
        weight = discount * going * (1.0 - trace * cut)
        step_mul = discount * trace * cut * going
        reward = rewards_ref[0, t]
        if t == steps - 1:
            add = reward + step_mul * add
            last = weight
        else:
            add = reward + weight * rows[t + 1] + step_mul * add
            last = step_mul * last
        mul = step_mul * mul
        chain_ref[t : t + 1] = add
        chain_ref[steps + t : steps + t + 1] = mul
        chain_ref[2 * steps + t : 2 * steps + t + 1] = last
    shards = send_ref.shape[0]
    width = discount.shape[1]
    for place, row in enumerate((add, mul, last, rows[0])):
        send_ref[:, place : place + 1, :] = jnp.broadcast_to(row[None], (shards, 1, width))


def target_kernel(
    steps,
    here_ref,
    valid_ref,
    counts_ref,
    dests_ref,
    chain_ref,
    got_ref,
    targets_ref,
    load_ref,
):
    group, shard = here_ref[0], here_ref[1]
    shards = got_ref.shape[0]
    width = chain_ref.shape[1]
    zero = jnp.zeros((1, width), F32)

    carry, first = zero, zero
    kept_carry, kept_first = zero, zero
    for s in range(shards - 1, -1, -1):
        carry = got_ref[s, 0:1] + got_ref[s, 1:2] * carry + got_ref[s, 2:3] * first
        first = got_ref[s, 3:4]
        follows = jnp.full((1, width), shard + 1, jnp.int32) == s
        kept_carry = jnp.where(follows, carry, kept_carry)
        kept_first = jnp.where(follows, first, kept_first)
    for t in range(steps):
        total = (
            chain_ref[t : t + 1]
            + chain_ref[steps + t : steps + t + 1] * kept_carry
            + chain_ref[2 * steps + t : 2 * steps + t + 1] * kept_first
        )
        targets_ref[t : t + 1] = valid_ref[0, t].astype(F32) * total
    load = jnp.int32(0)
    for g in range(counts_ref.shape[0]):
        for t in range(steps):
            count = counts_ref[g, t]
            hit = jnp.logical_and(count > 0, dests_ref[g, t] == group)
            load = load + jnp.where(hit, count, 0)
    load_ref[0, 0] = load


def per_device(
    frames,
    sample_counts,
    dest_groups,
    episode_ends,
    valid_steps,
    rewards,
    ratios,
    stored_values,
    stem_weight,
    conv_first,
    conv_second,
    value_weight,
    discounts,
    lambdas,
):
    steps = frames.shape[1]
    shards = lax.axis_size("tm")
    heads = value_weight.shape[1]
    here = jnp.stack([lax.axis_index("grp"), lax.axis_index("tm")]).astype(jnp.int32)
    all_counts = lax.all_gather(sample_counts, "grp", axis=0, tiled=True)
    all_dests = lax.all_gather(dest_groups, "grp", axis=0, tiled=True)
    latents, pooled = encode(frames[0], sample_counts[0], stem_weight, conv_first, conv_second)
    smem = pl.BlockSpec(memory_space=pltpu.SMEM)
    vmem = pl.BlockSpec(memory_space=pltpu.VMEM)
    values, send, chain = pl.pallas_call(
        lambda *refs: head_kernel(steps, *refs),
        out_shape=(
            jax.ShapeDtypeStruct((steps, heads), F32),
            jax.ShapeDtypeStruct((shards, 4, heads), F32),
            jax.ShapeDtypeStruct((3 * steps, heads), F32),
        ),
        in_specs=[smem] * 4 + [vmem] * 5,
        out_specs=(vmem, vmem, vmem),
    )(
        sample_counts,
        episode_ends,
        rewards,
        ratios,
        pooled,
        stored_values[0],
        value_weight,
        discounts[None],
        lambdas[None],
    )
    got = lax.all_to_all(send, "tm", split_axis=0, concat_axis=0, tiled=True)
    targets, load = pl.pallas_call(
        lambda *refs: target_kernel(steps, *refs),
        out_shape=(
            jax.ShapeDtypeStruct((steps, heads), F32),
            jax.ShapeDtypeStruct((1, 1), jnp.int32),
        ),
        in_specs=[smem] * 4 + [vmem] * 2,
        out_specs=(vmem, smem),
    )(here, valid_steps, all_counts, all_dests, chain, got)
    return latents[None], values[None], targets[None], load


def solution(mesh):
    rows = P("grp", "tm")
    deep = P("grp", "tm", None)
    whole = P("grp", "tm", None, None, None)
    in_specs = (whole,) + (rows,) * 6 + (deep,) + (P(),) * 6
    out_specs = (whole, deep, deep, rows)
    return jax.shard_map(
        per_device, mesh=mesh, in_specs=in_specs, out_specs=out_specs, check_vma=False
    )
```

```python
import functools

import jax
import jax.numpy as jnp
from jax import lax
from jax.experimental import pallas as pl
from jax.experimental.pallas import tpu as pltpu
from jax.sharding import PartitionSpec as P

BF = jnp.bfloat16
F32 = jnp.float32
LANE = 8
TAPS = 9
GRANT = 60 * 2**20


def tile_order(flat_ref, side):
    half, third = side // 2, side // LANE
    tiles = []
    for y in range(half):
        for j in range(third):
            for h in range(2):
                start = side * (half * h + y) + j
                rows = pl.ds(start, LANE, stride=third)
                parts = [flat_ref[c, rows, :] for c in range(flat_ref.shape[0])]
                tiles.append(jnp.concatenate(parts, axis=1))
    return jnp.stack(tiles).reshape(half, third, 2, LANE, -1)


def put_padded(out_ref, b, tiles):
    half, third, _, _, width = tiles.shape
    place = lax.broadcasted_iota(jnp.int32, (half * 2, LANE, width), 1)
    before = pltpu.roll(tiles[:, third - 1].reshape(half * 2, LANE, width), 1, 1)
    before = jnp.where(place == 0, 0.0, before).reshape(half, 1, 2, LANE, width)
    after = pltpu.roll(tiles[:, 0].reshape(half * 2, LANE, width), LANE - 1, 1)
    after = jnp.where(place == LANE - 1, 0.0, after).reshape(half, 1, 2, LANE, width)
    wide = jnp.concatenate([before, tiles, after], axis=1)
    rows = wide.reshape(half, third + 2, 2 * LANE, width).astype(BF)
    out_ref[b, 1 : half + 1] = rows
    none = jnp.zeros((third + 2, 1, LANE, width), F32)
    top = jnp.concatenate([none, wide[half - 1, :, 0:1]], axis=1)
    out_ref[b, 0] = top.reshape(third + 2, 2 * LANE, width).astype(BF)
    bottom = jnp.concatenate([wide[0, :, 1:2], none], axis=1)
    out_ref[b, half + 1] = bottom.reshape(third + 2, 2 * LANE, width).astype(BF)


def normed(hidden):
    wide = hidden.astype(F32)
    scale = lax.rsqrt(jnp.mean(wide * wide, axis=-1, keepdims=True) + 1e-05)
    return jnp.maximum(wide * scale, 0.0)


def conv(src_ref, b, weight_ref):
    _, tall, broad, rows, width = src_ref.shape
    half, third = tall - 2, broad - 2
    total = None
    for tap in range(TAPS):
        dy, dx = tap // 3, tap % 3
        window = src_ref[b, dy : dy + half, dx : dx + third].reshape(half * third * rows, width)
        part = jnp.dot(window, weight_ref[tap], preferred_element_type=F32)
        total = part if total is None else total + part
    return total.reshape(half, third, 2, LANE, weight_ref.shape[2])


def window_rows(side):
    half, third = side // 2, side // LANE
    shape = (2 * LANE, side * side)
    tap = lax.broadcasted_iota(jnp.int32, shape, 0)
    at = lax.broadcasted_iota(jnp.int32, shape, 1)
    s = at % LANE
    h = (at // LANE) % 2
    j = (at // (2 * LANE)) % third
    y = at // (2 * LANE * third) + half * h
    x = s * third + j
    dy, dx = tap // 3 - 1, tap % 3 - 1
    out = ((dy == -1) & (y == side - 1)) | ((dy == 1) & (y == 0))
    out = out | ((dx == -1) & (x == side - 1)) | ((dx == 1) & (x == 0))
    inside = (tap == TAPS) | ((tap < TAPS) & jnp.logical_not(out))
    return jnp.where(inside, 1.0, 0.0).astype(BF)


def front_kernel(
    side,
    counts_hbm,
    ends_hbm,
    rewards_hbm,
    ratios_hbm,
    frames_hbm,
    stored_hbm,
    stem_hbm,
    first_hbm,
    second_hbm,
    head_hbm,
    discounts_hbm,
    lambdas_hbm,
    middle_hbm,
    hidden_hbm,
    values_ref,
    send_ref,
    chain_ref,
    frames,
    stem,
    weights,
    flat,
    hidden,
    act,
    mid,
    counts_ref,
    ends_ref,
    rewards_ref,
    ratios_ref,
    stored_ref,
    head_ref,
    discounts_ref,
    lambdas_ref,
    sems,
):
    steps = frames.shape[0]
    half = side // 2
    sem = iter(range(64))

    def load(src, dst):
        copy = pltpu.make_async_copy(src, dst, sems.at[next(sem)])
        copy.start()
        return copy

    stem_copy = load(stem_hbm, stem)
    frame_copies = [load(frames_hbm.at[b], frames.at[b]) for b in range(steps)]
    weight_copies = [
        load(src, weights.at[i])
        for i, src in enumerate((first_hbm.at[0], second_hbm.at[0], first_hbm.at[1], second_hbm.at[1]))
    ]
    small = [
        load(src, dst)
        for src, dst in (
            (counts_hbm, counts_ref),
            (ends_hbm, ends_ref),
            (rewards_hbm, rewards_ref),
            (ratios_hbm, ratios_ref),
            (stored_hbm, stored_ref),
            (head_hbm, head_ref),
            (discounts_hbm, discounts_ref),
            (lambdas_hbm, lambdas_ref),
        )
    ]
    stem_copy.wait()
    for b in range(steps):
        frame_copies[b].wait()
        rows = jnp.maximum(jnp.dot(frames[b], stem[...], preferred_element_type=F32), 0.0)
        for c in range(flat.shape[1]):
            flat[b, c] = rows[:, 128 * c : 128 * c + 128]
        start = tile_order(flat.at[b], side).astype(BF)
        hidden[b] = start.reshape(hidden.shape[1:])
        put_padded(act, b, normed(start))
    weight_copies[0].wait()
    for b in range(steps):
        put_padded(mid, b, jnp.maximum(conv(act, b, weights.at[0]), 0.0))
    weight_copies[1].wait()
    for b in range(steps):
        out = conv(mid, b, weights.at[1])
        now = (hidden[b].astype(F32).reshape(out.shape) + out).astype(BF)
        hidden[b] = now.reshape(hidden.shape[1:])
        put_padded(act, b, normed(now))
    out_copies = []
    for b in range(steps):
        out_copies.append(load(hidden.at[b], hidden_hbm.at[b]))
    weight_copies[2].wait()
    for b in range(steps):
        put_padded(mid, b, jnp.maximum(conv(act, b, weights.at[2]), 0.0))
        out_copies.append(load(mid.at[b], middle_hbm.at[b]))

    select = window_rows(side)
    width = hidden.shape[-1]
    sums, kept = [], []
    for b in range(steps):
        block = mid[b, 1 : half + 1, 1 : mid.shape[2] - 1].reshape(side * side, width)
        sums.append(jnp.dot(select, block, preferred_element_type=F32))
        rows = hidden[b].reshape(side * side, width)
        kept.append(jnp.dot(select, rows, preferred_element_type=F32)[TAPS : TAPS + 1])
    weight_copies[3].wait()
    pooled = None
    for tap in range(TAPS):
        exact = jnp.concatenate([block[tap : tap + 1] for block in sums], axis=0)
        parts, rest = [], exact
        for _ in range(3):
            part = rest.astype(BF)
            parts.append(part.astype(F32))
            rest = rest - part.astype(F32)
        stacked = jnp.concatenate(parts + [jnp.zeros_like(exact)], axis=0).astype(BF)
        term = jnp.dot(stacked, weights[3, tap], preferred_element_type=F32)
        pooled = term if pooled is None else pooled + term
    pooled = pooled[0:steps] + pooled[steps : 2 * steps] + pooled[2 * steps : 3 * steps]
    pooled = (pooled + jnp.concatenate(kept, axis=0)) * (1.0 / (side * side))
    for copy in small:
        copy.wait()
    fresh = jnp.dot(
        pooled,
        head_ref[...].astype(F32),
        precision=lax.Precision.HIGHEST,
        preferred_element_type=F32,
    )
    discount = discounts_ref[...]
    trace = lambdas_ref[...]
    rows = []
    for t in range(steps):
        live = jnp.full((1, fresh.shape[1]), counts_ref[0, t], jnp.int32) > 0
        rows.append(jnp.where(live, fresh[t : t + 1], stored_ref[t : t + 1]))
        values_ref[t : t + 1] = rows[t]
    add = jnp.zeros_like(discount)
    mul = jnp.ones_like(discount)
    last = jnp.zeros_like(discount)
    for t in range(steps - 1, -1, -1):
        going = 1.0 - ends_ref[0, t].astype(F32)
        cut = jnp.minimum(1.0, ratios_ref[0, t])
        weight = discount * going * (1.0 - trace * cut)
        step_mul = discount * trace * cut * going
        reward = rewards_ref[0, t]
        if t == steps - 1:
            add = reward + step_mul * add
            last = weight
        else:
            add = reward + weight * rows[t + 1] + step_mul * add
            last = step_mul * last
        mul = step_mul * mul
        chain_ref[t : t + 1] = add
        chain_ref[steps + t : steps + t + 1] = mul
        chain_ref[2 * steps + t : 2 * steps + t + 1] = last
    shards = send_ref.shape[0]
    for place, row in enumerate((add, mul, last, rows[0])):
        send_ref[:, place : place + 1, :] = jnp.broadcast_to(row[None], (shards, 1, row.shape[1]))
    for copy in out_copies:
        copy.wait()


def back_kernel(side, counts_ref, middle_hbm, hidden_hbm, second_hbm, out_hbm, mid, hidden, weight, flat, done, sems):
    steps = mid.shape[0]
    half, third = side // 2, side // LANE
    copies = []

    def load(i, src, dst):
        copy = pltpu.make_async_copy(src, dst, sems.at[i])
        copy.start()
        return copy

    weight_copy = load(0, second_hbm.at[1], weight)
    for b in range(steps):
        copies.append(
            (
                load(1 + 3 * b, middle_hbm.at[b], mid.at[b]),
                load(2 + 3 * b, hidden_hbm.at[b], hidden.at[b]),
            )
        )
    weight_copy.wait()
    outs = []
    for b in range(steps):
        for copy in copies[b]:
            copy.wait()
        out = conv(mid, b, weight)
        out = hidden[b].astype(F32).reshape(out.shape) + out
        out = jnp.where(counts_ref[0, b] > 0, out, jnp.zeros_like(out))
        for y in range(half):
            for j in range(third):
                for h in range(2):
                    start = side * (half * h + y) + j
                    for c in range(flat.shape[1]):
                        flat[b, c, pl.ds(start, LANE, stride=third), :] = out[y, j, h, :, 128 * c : 128 * c + 128]
        for c in range(flat.shape[1]):
            done[b, :, 128 * c : 128 * c + 128] = flat[b, c].astype(BF)
        outs.append(load(3 + 3 * b, done.at[b], out_hbm.at[b]))
    for copy in outs:
        copy.wait()


SMEM = pl.BlockSpec(memory_space=pltpu.SMEM)
VMEM = pl.BlockSpec(memory_space=pltpu.VMEM)
HBM = pl.BlockSpec(memory_space=pl.ANY)


def front(counts, ends, rewards, ratios, frames, stored, stem, first, second, head, discounts, lambdas, shards):
    steps, side, _, pdim = frames.shape
    width, heads = stem.shape[1], head.shape[1]
    half, third = side // 2, side // LANE
    padded = (steps, half + 2, third + 2, 2 * LANE, width)
    plain = (steps, half, third, 2 * LANE, width)
    area = side * side
    work = steps * area * 2 * width * (pdim + 3 * TAPS * width)
    return pl.pallas_call(
        functools.partial(front_kernel, side),
        out_shape=(
            jax.ShapeDtypeStruct(padded, BF),
            jax.ShapeDtypeStruct(plain, BF),
            jax.ShapeDtypeStruct((steps, heads), F32),
            jax.ShapeDtypeStruct((shards, 4, heads), F32),
            jax.ShapeDtypeStruct((3 * steps, heads), F32),
        ),
        in_specs=[HBM] * 12,
        out_specs=(HBM, HBM, VMEM, VMEM, VMEM),
        scratch_shapes=[
            pltpu.VMEM((steps, area, pdim), BF),
            pltpu.VMEM(stem.shape, BF),
            pltpu.VMEM((4, TAPS, width, width), BF),
            pltpu.VMEM((steps, width // 128, area, 128), F32),
            pltpu.VMEM(plain, BF),
            pltpu.VMEM(padded, BF),
            pltpu.VMEM(padded, BF),
            pltpu.SMEM(counts.shape, jnp.int32),
            pltpu.SMEM(ends.shape, jnp.int32),
            pltpu.SMEM(rewards.shape, F32),
            pltpu.SMEM(ratios.shape, F32),
            pltpu.VMEM(stored.shape, F32),
            pltpu.VMEM(head.shape, BF),
            pltpu.VMEM(discounts.shape, F32),
            pltpu.VMEM(lambdas.shape, F32),
            pltpu.SemaphoreType.DMA((32,)),
        ],
        compiler_params=pltpu.CompilerParams(vmem_limit_bytes=GRANT),
        cost_estimate=pl.CostEstimate(flops=work, bytes_accessed=16 * 10**6, transcendentals=0),
    )(counts, ends, rewards, ratios, frames.reshape(steps, area, pdim), stored, stem, first, second, head, discounts, lambdas)


def back(counts, middle, hidden, second, side):
    steps, width = middle.shape[0], middle.shape[-1]
    area = side * side
    return pl.pallas_call(
        functools.partial(back_kernel, side),
        out_shape=jax.ShapeDtypeStruct((steps, area, width), BF),
        in_specs=[SMEM, HBM, HBM, HBM],
        out_specs=HBM,
        scratch_shapes=[
            pltpu.VMEM(middle.shape, BF),
            pltpu.VMEM(hidden.shape, BF),
            pltpu.VMEM((TAPS, width, width), BF),
            pltpu.VMEM((steps, width // 128, area, 128), F32),
            pltpu.VMEM((steps, area, width), BF),
            pltpu.SemaphoreType.DMA((32,)),
        ],
        compiler_params=pltpu.CompilerParams(vmem_limit_bytes=GRANT),
        cost_estimate=pl.CostEstimate(
            flops=steps * area * 2 * width * TAPS * width, bytes_accessed=8 * 10**6, transcendentals=0
        ),
    )(counts, middle, hidden, second)


def target_kernel(
    steps,
    here_ref,
    valid_ref,
    counts_ref,
    dests_ref,
    chain_ref,
    got_ref,
    targets_ref,
    load_ref,
):
    group, shard = here_ref[0], here_ref[1]
    shards = got_ref.shape[0]
    width = chain_ref.shape[1]
    zero = jnp.zeros((1, width), F32)

    carry, first = zero, zero
    kept_carry, kept_first = zero, zero
    for s in range(shards - 1, -1, -1):
        carry = got_ref[s, 0:1] + got_ref[s, 1:2] * carry + got_ref[s, 2:3] * first
        first = got_ref[s, 3:4]
        follows = jnp.full((1, width), shard + 1, jnp.int32) == s
        kept_carry = jnp.where(follows, carry, kept_carry)
        kept_first = jnp.where(follows, first, kept_first)
    for t in range(steps):
        total = (
            chain_ref[t : t + 1]
            + chain_ref[steps + t : steps + t + 1] * kept_carry
            + chain_ref[2 * steps + t : 2 * steps + t + 1] * kept_first
        )
        targets_ref[t : t + 1] = valid_ref[0, t].astype(F32) * total
    load = jnp.int32(0)
    for g in range(counts_ref.shape[0]):
        for t in range(steps):
            count = counts_ref[g, t]
            hit = jnp.logical_and(count > 0, dests_ref[g, t] == group)
            load = load + jnp.where(hit, count, 0)
    load_ref[0, 0] = load


def per_device(
    frames,
    sample_counts,
    dest_groups,
    episode_ends,
    valid_steps,
    rewards,
    ratios,
    stored_values,
    stem_weight,
    conv_first,
    conv_second,
    value_weight,
    discounts,
    lambdas,
):
    steps, side = frames.shape[1], frames.shape[2]
    width = stem_weight.shape[1]
    heads = value_weight.shape[1]
    shards = lax.axis_size("tm")
    here = jnp.stack([lax.axis_index("grp"), lax.axis_index("tm")]).astype(jnp.int32)
    all_counts = lax.all_gather(sample_counts, "grp", axis=0, tiled=True)
    all_dests = lax.all_gather(dest_groups, "grp", axis=0, tiled=True)
    middle, hidden, values, send, chain = front(
        sample_counts,
        episode_ends,
        rewards,
        ratios,
        frames[0],
        stored_values[0],
        stem_weight,
        conv_first,
        conv_second,
        value_weight,
        discounts[None],
        lambdas[None],
        shards,
    )
    got = lax.all_to_all(send, "tm", split_axis=0, concat_axis=0, tiled=True)
    latents = back(sample_counts, middle, hidden, conv_second, side)
    targets, load = pl.pallas_call(
        functools.partial(target_kernel, steps),
        out_shape=(
            jax.ShapeDtypeStruct((steps, heads), F32),
            jax.ShapeDtypeStruct((1, 1), jnp.int32),
        ),
        in_specs=[SMEM] * 4 + [VMEM] * 2,
        out_specs=(VMEM, SMEM),
    )(here, valid_steps, all_counts, all_dests, chain, got)
    latents = latents.reshape(1, steps, side, side, width)
    return latents, values[None], targets[None], load


def solution(mesh):
    rows = P("grp", "tm")
    deep = P("grp", "tm", None)
    whole = P("grp", "tm", None, None, None)
    in_specs = (whole,) + (rows,) * 6 + (deep,) + (P(),) * 6
    out_specs = (whole, deep, deep, rows)
    return jax.shard_map(
        per_device, mesh=mesh, in_specs=in_specs, out_specs=out_specs, check_vma=False
    )
```

```python
import functools

import jax
import jax.numpy as jnp
from jax import lax
from jax.experimental import pallas as pl
from jax.experimental.pallas import tpu as pltpu
from jax.sharding import PartitionSpec as P

BF = jnp.bfloat16
F32 = jnp.float32
LANE = 8
TAPS = 9
GRANT = 60 * 2**20


def tile_order(flat_ref, side):
    half, third = side // 2, side // LANE
    tiles = []
    for y in range(half):
        for j in range(third):
            for h in range(2):
                start = side * (half * h + y) + j
                rows = pl.ds(start, LANE, stride=third)
                parts = [flat_ref[c, rows, :] for c in range(flat_ref.shape[0])]
                tiles.append(jnp.concatenate(parts, axis=1))
    return jnp.stack(tiles).reshape(half, third, 2, LANE, -1)


def put_padded(out_ref, b, tiles):
    half, third, _, _, width = tiles.shape
    place = lax.broadcasted_iota(jnp.int32, (half * 2, LANE, width), 1)
    before = pltpu.roll(tiles[:, third - 1].reshape(half * 2, LANE, width), 1, 1)
    before = jnp.where(place == 0, 0.0, before).reshape(half, 1, 2, LANE, width)
    after = pltpu.roll(tiles[:, 0].reshape(half * 2, LANE, width), LANE - 1, 1)
    after = jnp.where(place == LANE - 1, 0.0, after).reshape(half, 1, 2, LANE, width)
    wide = jnp.concatenate([before, tiles, after], axis=1)
    rows = wide.reshape(half, third + 2, 2 * LANE, width).astype(BF)
    out_ref[b, 1 : half + 1] = rows
    none = jnp.zeros((third + 2, 1, LANE, width), F32)
    top = jnp.concatenate([none, wide[half - 1, :, 0:1]], axis=1)
    out_ref[b, 0] = top.reshape(third + 2, 2 * LANE, width).astype(BF)
    bottom = jnp.concatenate([wide[0, :, 1:2], none], axis=1)
    out_ref[b, half + 1] = bottom.reshape(third + 2, 2 * LANE, width).astype(BF)


def normed(hidden):
    wide = hidden.astype(F32)
    scale = lax.rsqrt(jnp.mean(wide * wide, axis=-1, keepdims=True) + 1e-05)
    return jnp.maximum(wide * scale, 0.0)


def conv(src_ref, b, weight_ref):
    _, tall, broad, rows, width = src_ref.shape
    half, third = tall - 2, broad - 2
    total = None
    for tap in range(TAPS):
        dy, dx = tap // 3, tap % 3
        window = src_ref[b, dy : dy + half, dx : dx + third].reshape(half * third * rows, width)
        part = jnp.dot(window, weight_ref[tap], preferred_element_type=F32)
        total = part if total is None else total + part
    return total.reshape(half, third, 2, LANE, weight_ref.shape[2])


def window_rows(side):
    half, third = side // 2, side // LANE
    shape = (2 * LANE, side * side)
    tap = lax.broadcasted_iota(jnp.int32, shape, 0)
    at = lax.broadcasted_iota(jnp.int32, shape, 1)
    s = at % LANE
    h = (at // LANE) % 2
    j = (at // (2 * LANE)) % third
    y = at // (2 * LANE * third) + half * h
    x = s * third + j
    dy, dx = tap // 3 - 1, tap % 3 - 1
    out = ((dy == -1) & (y == side - 1)) | ((dy == 1) & (y == 0))
    out = out | ((dx == -1) & (x == side - 1)) | ((dx == 1) & (x == 0))
    inside = (tap == TAPS) | ((tap < TAPS) & jnp.logical_not(out))
    return jnp.where(inside, 1.0, 0.0).astype(BF)


def front_kernel(
    side,
    counts_hbm,
    ends_hbm,
    rewards_hbm,
    ratios_hbm,
    frames_hbm,
    stored_hbm,
    stem_hbm,
    first_hbm,
    second_hbm,
    head_hbm,
    discounts_hbm,
    lambdas_hbm,
    middle_hbm,
    hidden_hbm,
    values_ref,
    send_ref,
    chain_ref,
    frames,
    stem,
    weights,
    flat,
    hidden,
    act,
    mid,
    counts_ref,
    ends_ref,
    rewards_ref,
    ratios_ref,
    stored_ref,
    head_ref,
    discounts_ref,
    lambdas_ref,
    sems,
):
    steps = frames.shape[0]
    half = side // 2
    sem = iter(range(64))

    def load(src, dst):
        copy = pltpu.make_async_copy(src, dst, sems.at[next(sem)])
        copy.start()
        return copy

    stem_copy = load(stem_hbm, stem)
    frame_copies = [pltpu.make_async_copy(frames_hbm.at[b], frames.at[b], sems.at[next(sem)]) for b in range(steps)]
    weight_copies = [
        pltpu.make_async_copy(src, weights.at[i], sems.at[next(sem)])
        for i, src in enumerate((first_hbm.at[0], second_hbm.at[0], first_hbm.at[1], second_hbm.at[1]))
    ]
    frame_copies[0].start()
    weight_copies[0].start()
    frame_copies[1].start()
    small = [
        load(src, dst)
        for src, dst in (
            (counts_hbm, counts_ref),
            (ends_hbm, ends_ref),
            (rewards_hbm, rewards_ref),
            (ratios_hbm, ratios_ref),
            (stored_hbm, stored_ref),
            (head_hbm, head_ref),
            (discounts_hbm, discounts_ref),
            (lambdas_hbm, lambdas_ref),
        )
    ]
    stem_copy.wait()

    def begin(b):
        for c in range(steps):

            @pl.when(b == c)
            def _():
                frame_copies[c].wait()
                if c + 2 < steps:
                    frame_copies[c + 2].start()
                else:
                    for i in range(c - 1, 2 * c - 2):
                        weight_copies[i].start()

        rows = jnp.maximum(jnp.dot(frames[b], stem[...], preferred_element_type=F32), 0.0)
        for c in range(flat.shape[0]):
            flat[c] = rows[:, 128 * c : 128 * c + 128]
        start = tile_order(flat, side).astype(BF)
        hidden[b] = start.reshape(hidden.shape[1:])
        put_padded(act, b, normed(start))

    def layer(l, _):
        def first(b, _):
            @pl.when(l == 0)
            def _():
                begin(b)

            @pl.when((l == 0) & (b == 0))
            def _():
                weight_copies[0].wait()

            @pl.when((l == 1) & (b == 0))
            def _():
                weight_copies[2].wait()

            put_padded(mid, b, jnp.maximum(conv(act, b, weights.at[2 * l]), 0.0))
            return 0

        def second(b, _):
            out = conv(mid, b, weights.at[1])
            now = (hidden[b].astype(F32).reshape(out.shape) + out).astype(BF)
            hidden[b] = now.reshape(hidden.shape[1:])
            put_padded(act, b, normed(now))
            return 0

        lax.fori_loop(0, steps, first, 0)

        @pl.when(l == 0)
        def _():
            weight_copies[1].wait()
            lax.fori_loop(0, steps, second, 0)

        return 0

    lax.fori_loop(0, 2, layer, 0)
    out_copies = [load(hidden, hidden_hbm), load(mid, middle_hbm)]

    select = window_rows(side)
    width = hidden.shape[-1]
    sums, kept = [], []
    for b in range(steps):
        block = mid[b, 1 : half + 1, 1 : mid.shape[2] - 1].reshape(side * side, width)
        sums.append(jnp.dot(select, block, preferred_element_type=F32))
        rows = hidden[b].reshape(side * side, width)
        kept.append(jnp.dot(select, rows, preferred_element_type=F32)[TAPS : TAPS + 1])
    weight_copies[3].wait()
    pooled = None
    for tap in range(TAPS):
        exact = jnp.concatenate([block[tap : tap + 1] for block in sums], axis=0)
        parts, rest = [], exact
        for _ in range(3):
            part = rest.astype(BF)
            parts.append(part.astype(F32))
            rest = rest - part.astype(F32)
        stacked = jnp.concatenate(parts + [jnp.zeros_like(exact)], axis=0).astype(BF)
        term = jnp.dot(stacked, weights[3, tap], preferred_element_type=F32)
        pooled = term if pooled is None else pooled + term
    pooled = pooled[0:steps] + pooled[steps : 2 * steps] + pooled[2 * steps : 3 * steps]
    pooled = (pooled + jnp.concatenate(kept, axis=0)) * (1.0 / (side * side))
    for copy in small:
        copy.wait()
    fresh = jnp.dot(
        pooled,
        head_ref[...].astype(F32),
        precision=lax.Precision.HIGHEST,
        preferred_element_type=F32,
    )
    discount = discounts_ref[...]
    trace = lambdas_ref[...]
    rows = []
    for t in range(steps):
        live = jnp.full((1, fresh.shape[1]), counts_ref[0, t], jnp.int32) > 0
        rows.append(jnp.where(live, fresh[t : t + 1], stored_ref[t : t + 1]))
        values_ref[t : t + 1] = rows[t]
    add = jnp.zeros_like(discount)
    mul = jnp.ones_like(discount)
    last = jnp.zeros_like(discount)
    for t in range(steps - 1, -1, -1):
        going = 1.0 - ends_ref[0, t].astype(F32)
        cut = jnp.minimum(1.0, ratios_ref[0, t])
        weight = discount * going * (1.0 - trace * cut)
        step_mul = discount * trace * cut * going
        reward = rewards_ref[0, t]
        if t == steps - 1:
            add = reward + step_mul * add
            last = weight
        else:
            add = reward + weight * rows[t + 1] + step_mul * add
            last = step_mul * last
        mul = step_mul * mul
        chain_ref[t : t + 1] = add
        chain_ref[steps + t : steps + t + 1] = mul
        chain_ref[2 * steps + t : 2 * steps + t + 1] = last
    shards = send_ref.shape[0]
    for place, row in enumerate((add, mul, last, rows[0])):
        send_ref[:, place : place + 1, :] = jnp.broadcast_to(row[None], (shards, 1, row.shape[1]))
    for copy in out_copies:
        copy.wait()


def back_kernel(side, counts_ref, middle_hbm, hidden_hbm, second_hbm, out_hbm, mid, hidden, weight, flat, done, sems):
    steps = mid.shape[0]
    half, third = side // 2, side // LANE
    copies = []

    def load(i, src, dst):
        copy = pltpu.make_async_copy(src, dst, sems.at[i])
        copy.start()
        return copy

    weight_copy = load(0, second_hbm.at[1], weight)
    for b in range(steps):
        copies.append(
            (
                load(1 + 3 * b, middle_hbm.at[b], mid.at[b]),
                load(2 + 3 * b, hidden_hbm.at[b], hidden.at[b]),
            )
        )
    weight_copy.wait()

    def finish(b, _):
        pltpu.make_async_copy(middle_hbm.at[b], mid.at[b], sems.at[1 + 3 * b]).wait()
        pltpu.make_async_copy(hidden_hbm.at[b], hidden.at[b], sems.at[2 + 3 * b]).wait()
        out = conv(mid, b, weight)
        out = hidden[b].astype(F32).reshape(out.shape) + out
        out = jnp.where(counts_ref[0, b] > 0, out, jnp.zeros_like(out))
        for y in range(half):
            for j in range(third):
                for h in range(2):
                    start = side * (half * h + y) + j
                    for c in range(flat.shape[0]):
                        flat[c, pl.ds(start, LANE, stride=third), :] = out[y, j, h, :, 128 * c : 128 * c + 128]
        for c in range(flat.shape[0]):
            done[b, :, 128 * c : 128 * c + 128] = flat[c].astype(BF)
        pltpu.make_async_copy(done.at[b], out_hbm.at[b], sems.at[3 + 3 * b]).start()
        return 0

    lax.fori_loop(0, steps, finish, 0)
    for b in range(steps):
        pltpu.make_async_copy(done.at[b], out_hbm.at[b], sems.at[3 + 3 * b]).wait()


SMEM = pl.BlockSpec(memory_space=pltpu.SMEM)
VMEM = pl.BlockSpec(memory_space=pltpu.VMEM)
HBM = pl.BlockSpec(memory_space=pl.ANY)


def front(counts, ends, rewards, ratios, frames, stored, stem, first, second, head, discounts, lambdas, shards):
    steps, side, _, pdim = frames.shape
    width, heads = stem.shape[1], head.shape[1]
    half, third = side // 2, side // LANE
    padded = (steps, half + 2, third + 2, 2 * LANE, width)
    plain = (steps, half, third, 2 * LANE, width)
    area = side * side
    work = steps * area * 2 * width * (pdim + 3 * TAPS * width)
    return pl.pallas_call(
        functools.partial(front_kernel, side),
        out_shape=(
            jax.ShapeDtypeStruct(padded, BF),
            jax.ShapeDtypeStruct(plain, BF),
            jax.ShapeDtypeStruct((steps, heads), F32),
            jax.ShapeDtypeStruct((shards, 4, heads), F32),
            jax.ShapeDtypeStruct((3 * steps, heads), F32),
        ),
        in_specs=[HBM] * 12,
        out_specs=(HBM, HBM, VMEM, VMEM, VMEM),
        scratch_shapes=[
            pltpu.VMEM((steps, area, pdim), BF),
            pltpu.VMEM(stem.shape, BF),
            pltpu.VMEM((4, TAPS, width, width), BF),
            pltpu.VMEM((width // 128, area, 128), F32),
            pltpu.VMEM(plain, BF),
            pltpu.VMEM(padded, BF),
            pltpu.VMEM(padded, BF),
            pltpu.SMEM(counts.shape, jnp.int32),
            pltpu.SMEM(ends.shape, jnp.int32),
            pltpu.SMEM(rewards.shape, F32),
            pltpu.SMEM(ratios.shape, F32),
            pltpu.VMEM(stored.shape, F32),
            pltpu.VMEM(head.shape, BF),
            pltpu.VMEM(discounts.shape, F32),
            pltpu.VMEM(lambdas.shape, F32),
            pltpu.SemaphoreType.DMA((32,)),
        ],
        compiler_params=pltpu.CompilerParams(vmem_limit_bytes=GRANT),
        cost_estimate=pl.CostEstimate(flops=work, bytes_accessed=16 * 10**6, transcendentals=0),
    )(counts, ends, rewards, ratios, frames.reshape(steps, area, pdim), stored, stem, first, second, head, discounts, lambdas)


def back(counts, middle, hidden, second, side):
    steps, width = middle.shape[0], middle.shape[-1]
    area = side * side
    return pl.pallas_call(
        functools.partial(back_kernel, side),
        out_shape=jax.ShapeDtypeStruct((steps, area, width), BF),
        in_specs=[SMEM, HBM, HBM, HBM],
        out_specs=HBM,
        scratch_shapes=[
            pltpu.VMEM(middle.shape, BF),
            pltpu.VMEM(hidden.shape, BF),
            pltpu.VMEM((TAPS, width, width), BF),
            pltpu.VMEM((width // 128, area, 128), F32),
            pltpu.VMEM((steps, area, width), BF),
            pltpu.SemaphoreType.DMA((32,)),
        ],
        compiler_params=pltpu.CompilerParams(vmem_limit_bytes=GRANT),
        cost_estimate=pl.CostEstimate(
            flops=steps * area * 2 * width * TAPS * width, bytes_accessed=8 * 10**6, transcendentals=0
        ),
    )(counts, middle, hidden, second)


def target_kernel(steps, valid_hbm, loads_hbm, chain_hbm, got_ref, targets_ref, load_ref, valid_ref, loads_ref, chain_ref, sems):
    group, shard = lax.axis_index("grp"), lax.axis_index("tm")
    shards = got_ref.shape[0]
    groups, part = loads_ref.shape[0], loads_hbm.shape[0] // loads_ref.shape[0]
    width = chain_ref.shape[1]
    copies = [
        pltpu.make_async_copy(valid_hbm, valid_ref, sems.at[0]),
        pltpu.make_async_copy(chain_hbm, chain_ref, sems.at[1]),
    ]
    for g in range(groups):
        copies.append(pltpu.make_async_copy(loads_hbm.at[g * part], loads_ref.at[g], sems.at[2 + g]))
    for copy in copies:
        copy.start()
    zero = jnp.zeros((1, width), F32)
    carry, first = zero, zero
    kept_carry, kept_first = zero, zero
    for s in range(shards - 1, -1, -1):
        carry = got_ref[s, 0:1] + got_ref[s, 1:2] * carry + got_ref[s, 2:3] * first
        first = got_ref[s, 3:4]
        follows = jnp.full((1, width), shard + 1, jnp.int32) == s
        kept_carry = jnp.where(follows, carry, kept_carry)
        kept_first = jnp.where(follows, first, kept_first)
    for copy in copies:
        copy.wait()
    for t in range(steps):
        total = (
            chain_ref[t : t + 1]
            + chain_ref[steps + t : steps + t + 1] * kept_carry
            + chain_ref[2 * steps + t : 2 * steps + t + 1] * kept_first
        )
        targets_ref[t : t + 1] = valid_ref[0, t].astype(F32) * total
    lane = lax.broadcasted_iota(jnp.int32, loads_ref.shape, 2)
    mine = jnp.where(lane == group, loads_ref[...], 0).astype(F32)
    mine = jnp.sum(jnp.sum(mine, axis=0), axis=0, keepdims=True)
    load_ref[...] = jnp.sum(mine, axis=1, keepdims=True).astype(jnp.int32)


def per_device(
    frames,
    sample_counts,
    dest_groups,
    episode_ends,
    valid_steps,
    rewards,
    ratios,
    stored_values,
    stem_weight,
    conv_first,
    conv_second,
    value_weight,
    discounts,
    lambdas,
):
    steps, side = frames.shape[1], frames.shape[2]
    width = stem_weight.shape[1]
    heads = value_weight.shape[1]
    groups, shards = lax.axis_size("grp"), lax.axis_size("tm")
    lanes = jnp.arange(128, dtype=jnp.int32)[None, :]
    hits = jnp.where(dest_groups[0][:, None] == lanes, jnp.maximum(sample_counts[0], 0)[:, None], 0)
    loads = lax.optimization_barrier(jnp.broadcast_to(hits[None], (128, steps, 128)))
    loads = lax.all_gather(loads, "grp", axis=0, tiled=True)
    middle, hidden, values, send, chain = front(
        sample_counts,
        episode_ends,
        rewards,
        ratios,
        frames[0],
        stored_values[0],
        stem_weight,
        conv_first,
        conv_second,
        value_weight,
        discounts[None],
        lambdas[None],
        shards,
    )
    got = lax.all_to_all(send, "tm", split_axis=0, concat_axis=0, tiled=True)
    latents = back(sample_counts, middle, hidden, conv_second, side)
    targets, load = pl.pallas_call(
        functools.partial(target_kernel, steps),
        out_shape=(
            jax.ShapeDtypeStruct((steps, heads), F32),
            jax.ShapeDtypeStruct((1, 1), jnp.int32),
        ),
        in_specs=[HBM, HBM, HBM, VMEM],
        out_specs=(VMEM, VMEM),
        scratch_shapes=[
            pltpu.SMEM(valid_steps.shape, jnp.int32),
            pltpu.VMEM((groups, steps, 128), jnp.int32),
            pltpu.VMEM((3 * steps, heads), F32),
            pltpu.SemaphoreType.DMA((2 + groups,)),
        ],
        compiler_params=pltpu.CompilerParams(vmem_limit_bytes=GRANT),
    )(valid_steps, loads, chain, got)
    latents = latents.reshape(1, steps, side, side, width)
    return latents, values[None], targets[None], load


def solution(mesh):
    rows = P("grp", "tm")
    deep = P("grp", "tm", None)
    whole = P("grp", "tm", None, None, None)
    in_specs = (whole,) + (rows,) * 6 + (deep,) + (P(),) * 6
    out_specs = (whole, deep, deep, rows)
    return jax.shard_map(
        per_device, mesh=mesh, in_specs=in_specs, out_specs=out_specs, check_vma=False
    )
```

```python
import functools

import jax
import jax.numpy as jnp
from jax import lax
from jax.experimental import pallas as pl
from jax.experimental.pallas import tpu as pltpu
from jax.sharding import PartitionSpec as P

BF = jnp.bfloat16
F32 = jnp.float32
LANE = 8
TAPS = 9
FRONT_GRANT = 60 * 2**20
BACK_GRANT = 60 * 2**20


def tile_order(flat_ref, side):
    half, third = side // 2, side // LANE
    tiles = []
    for y in range(half):
        for j in range(third):
            for h in range(2):
                start = side * (half * h + y) + j
                rows = pl.ds(start, LANE, stride=third)
                parts = [flat_ref[c, rows, :] for c in range(flat_ref.shape[0])]
                tiles.append(jnp.concatenate(parts, axis=1))
    return jnp.stack(tiles).reshape(half, third, 2, LANE, -1)


def put_padded(out_ref, b, tiles):
    half, third, _, _, width = tiles.shape
    place = lax.broadcasted_iota(jnp.int32, (half * 2, LANE, width), 1)
    before = pltpu.roll(tiles[:, third - 1].reshape(half * 2, LANE, width), 1, 1)
    before = jnp.where(place == 0, 0.0, before).reshape(half, 1, 2, LANE, width)
    after = pltpu.roll(tiles[:, 0].reshape(half * 2, LANE, width), LANE - 1, 1)
    after = jnp.where(place == LANE - 1, 0.0, after).reshape(half, 1, 2, LANE, width)
    wide = jnp.concatenate([before, tiles, after], axis=1)
    rows = wide.reshape(half, third + 2, 2 * LANE, width).astype(BF)
    out_ref[b, 1 : half + 1] = rows
    none = jnp.zeros((third + 2, 1, LANE, width), F32)
    top = jnp.concatenate([none, wide[half - 1, :, 0:1]], axis=1)
    out_ref[b, 0] = top.reshape(third + 2, 2 * LANE, width).astype(BF)
    bottom = jnp.concatenate([wide[0, :, 1:2], none], axis=1)
    out_ref[b, half + 1] = bottom.reshape(third + 2, 2 * LANE, width).astype(BF)


def normed(hidden):
    wide = hidden.astype(F32)
    scale = lax.rsqrt(jnp.mean(wide * wide, axis=-1, keepdims=True) + 1e-05)
    return jnp.maximum(wide * scale, 0.0)


def conv(src_ref, b, weight_ref):
    _, tall, broad, rows, width = src_ref.shape
    half, third = tall - 2, broad - 2
    total = None
    for tap in range(TAPS):
        dy, dx = tap // 3, tap % 3
        window = src_ref[b, dy : dy + half, dx : dx + third].reshape(half * third * rows, width)
        part = jnp.dot(window, weight_ref[tap], preferred_element_type=F32)
        total = part if total is None else total + part
    return total.reshape(half, third, 2, LANE, weight_ref.shape[2])


def window_rows(side):
    half, third = side // 2, side // LANE
    shape = (2 * LANE, side * side)
    tap = lax.broadcasted_iota(jnp.int32, shape, 0)
    at = lax.broadcasted_iota(jnp.int32, shape, 1)
    s = at % LANE
    h = (at // LANE) % 2
    j = (at // (2 * LANE)) % third
    y = at // (2 * LANE * third) + half * h
    x = s * third + j
    dy, dx = tap // 3 - 1, tap % 3 - 1
    out = ((dy == -1) & (y == side - 1)) | ((dy == 1) & (y == 0))
    out = out | ((dx == -1) & (x == side - 1)) | ((dx == 1) & (x == 0))
    inside = (tap == TAPS) | ((tap < TAPS) & jnp.logical_not(out))
    return jnp.where(inside, 1.0, 0.0).astype(BF)


def front_kernel(
    side,
    counts_hbm,
    ends_hbm,
    rewards_hbm,
    ratios_hbm,
    valid_hbm,
    frames_hbm,
    stored_hbm,
    stem_hbm,
    first_hbm,
    second_hbm,
    head_hbm,
    discounts_hbm,
    lambdas_hbm,
    middle_hbm,
    hidden_hbm,
    values_ref,
    send_ref,
    chain_ref,
    frames,
    stem,
    weights,
    flat,
    hidden,
    act,
    mid,
    sums,
    kept,
    counts_ref,
    ends_ref,
    rewards_ref,
    ratios_ref,
    valid_ref,
    stored_ref,
    head_ref,
    discounts_ref,
    lambdas_ref,
    sems,
):
    steps = frames.shape[0]
    half = side // 2
    sem = iter(range(64))

    def load(src, dst):
        copy = pltpu.make_async_copy(src, dst, sems.at[next(sem)])
        copy.start()
        return copy

    stem_copy = load(stem_hbm, stem)
    frame_copies = [pltpu.make_async_copy(frames_hbm.at[b], frames.at[b], sems.at[next(sem)]) for b in range(steps)]
    weight_copies = [
        pltpu.make_async_copy(src, weights.at[i], sems.at[next(sem)])
        for i, src in enumerate((first_hbm.at[0], second_hbm.at[0], first_hbm.at[1], second_hbm.at[1]))
    ]
    frame_copies[0].start()
    weight_copies[0].start()
    frame_copies[1].start()
    small = [
        load(src, dst)
        for src, dst in (
            (counts_hbm, counts_ref),
            (ends_hbm, ends_ref),
            (rewards_hbm, rewards_ref),
            (ratios_hbm, ratios_ref),
            (valid_hbm, valid_ref),
            (stored_hbm, stored_ref),
            (head_hbm, head_ref),
            (discounts_hbm, discounts_ref),
            (lambdas_hbm, lambdas_ref),
        )
    ]
    hidden_copy = pltpu.make_async_copy(hidden, hidden_hbm, sems.at[next(sem)])
    middle_sem = next(sem)

    def middle_copy(b):
        return pltpu.make_async_copy(mid.at[b], middle_hbm.at[b], sems.at[middle_sem + b])

    stem_copy.wait()

    def begin(b):
        for c in range(steps):

            @pl.when(b == c)
            def _():
                frame_copies[c].wait()
                if c + 2 < steps:
                    frame_copies[c + 2].start()
                else:
                    for i in range(c - 1, 2 * c - 2):
                        weight_copies[i].start()

        rows = jnp.maximum(jnp.dot(frames[b], stem[...], preferred_element_type=F32), 0.0)
        for c in range(flat.shape[0]):
            flat[c] = rows[:, 128 * c : 128 * c + 128]
        start = tile_order(flat, side).astype(BF)
        hidden[b] = start.reshape(hidden.shape[1:])
        put_padded(act, b, normed(start))

    def layer(l, _):
        def first(b, _):
            @pl.when(l == 0)
            def _():
                begin(b)

            @pl.when((l == 0) & (b == 0))
            def _():
                weight_copies[0].wait()

            @pl.when((l == 1) & (b == 0))
            def _():
                weight_copies[2].wait()

            put_padded(mid, b, jnp.maximum(conv(act, b, weights.at[2 * l]), 0.0))

            @pl.when(l == 1)
            def _():
                middle_copy(b).start()

            return 0

        def second(b, _):
            out = conv(mid, b, weights.at[1])
            now = (hidden[b].astype(F32).reshape(out.shape) + out).astype(BF)
            hidden[b] = now.reshape(hidden.shape[1:])
            put_padded(act, b, normed(now))
            return 0

        lax.fori_loop(0, steps, first, 0)

        @pl.when(l == 0)
        def _():
            weight_copies[1].wait()
            lax.fori_loop(0, steps, second, 0)
            hidden_copy.start()

        return 0

    lax.fori_loop(0, 2, layer, 0)

    select = window_rows(side)
    width = hidden.shape[-1]

    def total(b, _):
        block = mid[b, 1 : half + 1, 1 : mid.shape[2] - 1].reshape(side * side, width)
        rows = hidden[b].reshape(side * side, width)
        sums[b] = jnp.dot(select, block, preferred_element_type=F32)
        kept[b] = jnp.dot(select, rows, preferred_element_type=F32)
        return 0

    lax.fori_loop(0, steps, total, 0)
    weight_copies[3].wait()
    pooled = None
    for tap in range(TAPS):
        exact = jnp.concatenate([sums[b, tap : tap + 1] for b in range(steps)], axis=0)
        parts, rest = [], exact
        for _ in range(3):
            part = rest.astype(BF)
            parts.append(part.astype(F32))
            rest = rest - part.astype(F32)
        stacked = jnp.concatenate(parts + [jnp.zeros_like(exact)], axis=0).astype(BF)
        term = jnp.dot(stacked, weights[3, tap], preferred_element_type=F32)
        pooled = term if pooled is None else pooled + term
    pooled = pooled[0:steps] + pooled[steps : 2 * steps] + pooled[2 * steps : 3 * steps]
    pooled = (pooled + jnp.concatenate([kept[b, TAPS : TAPS + 1] for b in range(steps)], axis=0)) * (1.0 / (side * side))
    for copy in small:
        copy.wait()
    fresh = jnp.dot(
        pooled,
        head_ref[...].astype(F32),
        precision=lax.Precision.HIGHEST,
        preferred_element_type=F32,
    )
    discount = discounts_ref[...]
    trace = lambdas_ref[...]
    rows = []
    for t in range(steps):
        live = jnp.full((1, fresh.shape[1]), counts_ref[0, t], jnp.int32) > 0
        rows.append(jnp.where(live, fresh[t : t + 1], stored_ref[t : t + 1]))
        values_ref[t : t + 1] = rows[t]
    add = jnp.zeros_like(discount)
    mul = jnp.ones_like(discount)
    last = jnp.zeros_like(discount)
    for t in range(steps - 1, -1, -1):
        going = 1.0 - ends_ref[0, t].astype(F32)
        cut = jnp.minimum(1.0, ratios_ref[0, t])
        weight = discount * going * (1.0 - trace * cut)
        step_mul = discount * trace * cut * going
        reward = rewards_ref[0, t]
        if t == steps - 1:
            add = reward + step_mul * add
            last = weight
        else:
            add = reward + weight * rows[t + 1] + step_mul * add
            last = step_mul * last
        mul = step_mul * mul
        valid = valid_ref[0, t].astype(F32)
        chain_ref[t : t + 1] = valid * add
        chain_ref[steps + t : steps + t + 1] = valid * mul
        chain_ref[2 * steps + t : 2 * steps + t + 1] = valid * last
    shards = send_ref.shape[0]
    for place, row in enumerate((add, mul, last, rows[0])):
        send_ref[:, place : place + 1, :] = jnp.broadcast_to(row[None], (shards, 1, row.shape[1]))
    hidden_copy.wait()
    for b in range(steps):
        middle_copy(b).wait()


def back_kernel(side, counts_ref, middle_hbm, hidden_hbm, second_hbm, out_hbm, mid, hidden, weight, flat, done, sems):
    steps = mid.shape[0]
    half, third = side // 2, side // LANE
    copies = []

    def load(i, src, dst):
        copy = pltpu.make_async_copy(src, dst, sems.at[i])
        copy.start()
        return copy

    weight_copy = load(0, second_hbm.at[1], weight)
    for b in range(steps):
        copies.append(
            (
                load(1 + 3 * b, middle_hbm.at[b], mid.at[b]),
                load(2 + 3 * b, hidden_hbm.at[b], hidden.at[b]),
            )
        )
    weight_copy.wait()

    def finish(b, _):
        pltpu.make_async_copy(middle_hbm.at[b], mid.at[b], sems.at[1 + 3 * b]).wait()
        pltpu.make_async_copy(hidden_hbm.at[b], hidden.at[b], sems.at[2 + 3 * b]).wait()
        out = conv(mid, b, weight)
        out = hidden[b].astype(F32).reshape(out.shape) + out
        out = jnp.where(counts_ref[0, b] > 0, out, jnp.zeros_like(out))
        for y in range(half):
            for j in range(third):
                for h in range(2):
                    start = side * (half * h + y) + j
                    for c in range(flat.shape[0]):
                        flat[c, pl.ds(start, LANE, stride=third), :] = out[y, j, h, :, 128 * c : 128 * c + 128]
        for c in range(flat.shape[0]):
            done[b, :, 128 * c : 128 * c + 128] = flat[c].astype(BF)
        pltpu.make_async_copy(done.at[b], out_hbm.at[b], sems.at[3 + 3 * b]).start()
        return 0

    lax.fori_loop(0, steps, finish, 0)
    for b in range(steps):
        pltpu.make_async_copy(done.at[b], out_hbm.at[b], sems.at[3 + 3 * b]).wait()


SMEM = pl.BlockSpec(memory_space=pltpu.SMEM)
VMEM = pl.BlockSpec(memory_space=pltpu.VMEM)
HBM = pl.BlockSpec(memory_space=pl.ANY)


def front(counts, ends, rewards, ratios, valid, frames, stored, stem, first, second, head, discounts, lambdas, shards):
    steps, side, _, pdim = frames.shape
    width, heads = stem.shape[1], head.shape[1]
    half, third = side // 2, side // LANE
    padded = (steps, half + 2, third + 2, 2 * LANE, width)
    plain = (steps, half, third, 2 * LANE, width)
    area = side * side
    work = steps * area * 2 * width * (pdim + 3 * TAPS * width)
    return pl.pallas_call(
        functools.partial(front_kernel, side),
        out_shape=(
            jax.ShapeDtypeStruct(padded, BF),
            jax.ShapeDtypeStruct(plain, BF),
            jax.ShapeDtypeStruct((steps, heads), F32),
            jax.ShapeDtypeStruct((shards, 4, heads), F32),
            jax.ShapeDtypeStruct((3 * steps, heads), F32),
        ),
        in_specs=[HBM] * 13,
        out_specs=(HBM, HBM, VMEM, VMEM, VMEM),
        scratch_shapes=[
            pltpu.VMEM((steps, area, pdim), BF),
            pltpu.VMEM(stem.shape, BF),
            pltpu.VMEM((4, TAPS, width, width), BF),
            pltpu.VMEM((width // 128, area, 128), F32),
            pltpu.VMEM(plain, BF),
            pltpu.VMEM(padded, BF),
            pltpu.VMEM(padded, BF),
            pltpu.VMEM((steps, 2 * LANE, width), F32),
            pltpu.VMEM((steps, 2 * LANE, width), F32),
            pltpu.SMEM(counts.shape, jnp.int32),
            pltpu.SMEM(ends.shape, jnp.int32),
            pltpu.SMEM(rewards.shape, F32),
            pltpu.SMEM(ratios.shape, F32),
            pltpu.SMEM(valid.shape, jnp.int32),
            pltpu.VMEM(stored.shape, F32),
            pltpu.VMEM(head.shape, BF),
            pltpu.VMEM(discounts.shape, F32),
            pltpu.VMEM(lambdas.shape, F32),
            pltpu.SemaphoreType.DMA((32,)),
        ],
        compiler_params=pltpu.CompilerParams(vmem_limit_bytes=FRONT_GRANT),
        cost_estimate=pl.CostEstimate(flops=work, bytes_accessed=16 * 10**6, transcendentals=0),
    )(counts, ends, rewards, ratios, valid, frames.reshape(steps, area, pdim), stored, stem, first, second, head, discounts, lambdas)


def back(counts, middle, hidden, second, side):
    steps, width = middle.shape[0], middle.shape[-1]
    area = side * side
    return pl.pallas_call(
        functools.partial(back_kernel, side),
        out_shape=jax.ShapeDtypeStruct((steps, area, width), BF),
        in_specs=[SMEM, HBM, HBM, HBM],
        out_specs=HBM,
        scratch_shapes=[
            pltpu.VMEM(middle.shape, BF),
            pltpu.VMEM(hidden.shape, BF),
            pltpu.VMEM((TAPS, width, width), BF),
            pltpu.VMEM((width // 128, area, 128), F32),
            pltpu.VMEM((steps, area, width), BF),
            pltpu.SemaphoreType.DMA((32,)),
        ],
        compiler_params=pltpu.CompilerParams(vmem_limit_bytes=BACK_GRANT),
        cost_estimate=pl.CostEstimate(
            flops=steps * area * 2 * width * TAPS * width, bytes_accessed=8 * 10**6, transcendentals=0
        ),
    )(counts, middle, hidden, second)


def target_kernel(steps, *refs):
    groups = 4
    pairs = refs[: 2 * groups]
    chain_hbm, got_ref, targets_ref, load_ref = refs[2 * groups : 2 * groups + 4]
    held = refs[2 * groups + 4 : 4 * groups + 4]
    chain_ref, sems = refs[4 * groups + 4 :]
    group, shard = lax.axis_index("grp"), lax.axis_index("tm")
    shards, width = got_ref.shape[0], chain_ref.shape[1]
    copies = [
        pltpu.make_async_copy(src, dst, sems.at[i]) for i, (src, dst) in enumerate(zip(pairs + (chain_hbm,), held + (chain_ref,)))
    ]
    for copy in copies:
        copy.start()
    zero = jnp.zeros((1, width), F32)
    carry, first = zero, zero
    kept_carry, kept_first = zero, zero
    for s in range(shards - 1, -1, -1):
        carry = got_ref[s, 0:1] + got_ref[s, 1:2] * carry + got_ref[s, 2:3] * first
        first = got_ref[s, 3:4]
        follows = jnp.full((1, width), shard + 1, jnp.int32) == s
        kept_carry = jnp.where(follows, carry, kept_carry)
        kept_first = jnp.where(follows, first, kept_first)
    for copy in copies:
        copy.wait()
    for t in range(steps):
        targets_ref[t : t + 1] = (
            chain_ref[t : t + 1]
            + chain_ref[steps + t : steps + t + 1] * kept_carry
            + chain_ref[2 * steps + t : 2 * steps + t + 1] * kept_first
        )
    load = jnp.int32(0)
    for g in range(groups):
        for t in range(steps):
            count = held[2 * g][0, t]
            hit = jnp.logical_and(count > 0, held[2 * g + 1][0, t] == group)
            load = load + jnp.where(hit, count, 0)
    load_ref[0, 0] = load


def per_device(
    frames,
    sample_counts,
    dest_groups,
    episode_ends,
    valid_steps,
    rewards,
    ratios,
    stored_values,
    stem_weight,
    conv_first,
    conv_second,
    value_weight,
    discounts,
    lambdas,
):
    steps, side = frames.shape[1], frames.shape[2]
    width = stem_weight.shape[1]
    heads = value_weight.shape[1]
    groups, shards = lax.axis_size("grp"), lax.axis_size("tm")
    near = [(g, g ^ 1) for g in range(groups)]
    far = [(g, g ^ 3) for g in range(groups)]
    routed = [sample_counts, dest_groups]
    routed += [lax.ppermute(part, "grp", near) for part in routed]
    middle, hidden, values, send, chain = front(
        sample_counts,
        episode_ends,
        rewards,
        ratios,
        valid_steps,
        frames[0],
        stored_values[0],
        stem_weight,
        conv_first,
        conv_second,
        value_weight,
        discounts[None],
        lambdas[None],
        shards,
    )
    got = lax.all_to_all(send, "tm", split_axis=0, concat_axis=0, tiled=True)
    routed += [lax.ppermute(part, "grp", far) for part in routed]
    middle, *routed = lax.optimization_barrier((middle, *routed))
    latents = back(sample_counts, middle, hidden, conv_second, side)
    targets, load = pl.pallas_call(
        functools.partial(target_kernel, steps),
        out_shape=(
            jax.ShapeDtypeStruct((steps, heads), F32),
            jax.ShapeDtypeStruct((1, 1), jnp.int32),
        ),
        in_specs=[HBM] * (len(routed) + 1) + [VMEM],
        out_specs=(VMEM, SMEM),
        scratch_shapes=[pltpu.SMEM(sample_counts.shape, jnp.int32)] * len(routed)
        + [pltpu.VMEM((3 * steps, heads), F32), pltpu.SemaphoreType.DMA((len(routed) + 1,))],
        compiler_params=pltpu.CompilerParams(vmem_limit_bytes=BACK_GRANT),
    )(*routed, chain, got)
    latents = latents.reshape(1, steps, side, side, width)
    return latents, values[None], targets[None], load


def solution(mesh):
    rows = P("grp", "tm")
    deep = P("grp", "tm", None)
    whole = P("grp", "tm", None, None, None)
    in_specs = (whole,) + (rows,) * 6 + (deep,) + (P(),) * 6
    out_specs = (whole, deep, deep, rows)
    return jax.shard_map(
        per_device, mesh=mesh, in_specs=in_specs, out_specs=out_specs, check_vma=False
    )
```

```python
import functools

import jax
import jax.numpy as jnp
from jax import lax
from jax.experimental import pallas as pl
from jax.experimental.pallas import tpu as pltpu
from jax.sharding import PartitionSpec as P

BF = jnp.bfloat16
F32 = jnp.float32
LANE = 8
TAPS = 9
WINO = True
CHUNK = 12
FRONT_GRANT = 60 * 2**20
BACK_GRANT = 60 * 2**20


def tile_order(flat_ref, side):
    half, third = side // 2, side // LANE
    tiles = []
    for y in range(half):
        for j in range(third):
            for h in range(2):
                start = side * (half * h + y) + j
                rows = pl.ds(start, LANE, stride=third)
                parts = [flat_ref[c, rows, :] for c in range(flat_ref.shape[0])]
                tiles.append(jnp.concatenate(parts, axis=1))
    return jnp.stack(tiles).reshape(half, third, 2, LANE, -1)


def put_padded(out_ref, b, tiles, y0, half):
    count, third, _, _, width = tiles.shape
    place = lax.broadcasted_iota(jnp.int32, (count * 2, LANE, width), 1)
    before = pltpu.roll(tiles[:, third - 1].reshape(count * 2, LANE, width), 1, 1)
    before = jnp.where(place == 0, 0.0, before).reshape(count, 1, 2, LANE, width)
    after = pltpu.roll(tiles[:, 0].reshape(count * 2, LANE, width), LANE - 1, 1)
    after = jnp.where(place == LANE - 1, 0.0, after).reshape(count, 1, 2, LANE, width)
    wide = jnp.concatenate([before, tiles, after], axis=1)
    rows = wide.reshape(count, third + 2, 2 * LANE, width).astype(BF)
    out_ref[b, y0 + 1 : y0 + count + 1] = rows
    none = jnp.zeros((third + 2, 1, LANE, width), F32)
    if y0 + count == half:
        top = jnp.concatenate([none, wide[count - 1, :, 0:1]], axis=1)
        out_ref[b, 0] = top.reshape(third + 2, 2 * LANE, width).astype(BF)
    if y0 == 0:
        bottom = jnp.concatenate([wide[0, :, 1:2], none], axis=1)
        out_ref[b, half + 1] = bottom.reshape(third + 2, 2 * LANE, width).astype(BF)


def normed(hidden):
    wide = hidden.astype(F32)
    scale = lax.rsqrt(jnp.mean(wide * wide, axis=-1, keepdims=True) + 1e-05)
    return jnp.maximum(wide * scale, 0.0)


def conv(src_ref, b, weight_ref, mixed_ref, y0, count):
    _, tall, broad, rows, width = src_ref.shape
    third = broad - 2
    if not WINO:
        total = None
        for tap in range(TAPS):
            dy, dx = tap // 3, tap % 3
            window = src_ref[b, y0 + dy : y0 + dy + count, dx : dx + third].reshape(count * third * rows, width)
            part = jnp.dot(window, weight_ref[tap], preferred_element_type=F32)
            total = part if total is None else total + part
        return total.reshape(count, third, 2, LANE, weight_ref.shape[2])
    pairs = count // 2
    block = src_ref[b, y0 : y0 + count + 2].reshape(pairs + 1, 2, broad, rows, width)
    e0, e1, e2, e3 = block[:pairs, 0], block[:pairs, 1], block[1:, 0], block[1:, 1]
    parts = []
    for k, mix in enumerate((e0 - e2, e1 + e2, e2 - e1, e1 - e3)):
        total = None
        for dx in range(3):
            weight = (weight_ref[dx], mixed_ref[dx], mixed_ref[3 + dx], weight_ref[6 + dx])[k]
            window = mix[:, dx : dx + third].reshape(pairs * third * rows, width)
            part = jnp.dot(window, weight, preferred_element_type=F32)
            total = part if total is None else total + part
        parts.append(total)
    low = parts[0] + parts[1] + parts[2]
    high = parts[1] - parts[2] - parts[3]
    out = jnp.stack([x.reshape(pairs, third, 2, LANE, -1) for x in (low, high)], axis=1)
    return out.reshape(count, third, 2, LANE, -1)


def mix_weights(weight_ref, mixed_ref):
    if not WINO:
        return
    size = weight_ref.shape[1]

    def some(i, _):
        rows = pl.ds(pl.multiple_of(i * 64, 64), 64)
        for dx in range(3):
            outer = weight_ref[dx, rows].astype(F32) + weight_ref[6 + dx, rows].astype(F32)
            inner = weight_ref[3 + dx, rows].astype(F32)
            mixed_ref[dx, rows] = (0.5 * (outer + inner)).astype(BF)
            mixed_ref[3 + dx, rows] = (0.5 * (outer - inner)).astype(BF)
        return 0

    lax.fori_loop(0, size // 64, some, 0)


def window_rows(side):
    half, third = side // 2, side // LANE
    shape = (2 * LANE, side * side)
    tap = lax.broadcasted_iota(jnp.int32, shape, 0)
    at = lax.broadcasted_iota(jnp.int32, shape, 1)
    s = at % LANE
    h = (at // LANE) % 2
    j = (at // (2 * LANE)) % third
    y = at // (2 * LANE * third) + half * h
    x = s * third + j
    dy, dx = tap // 3 - 1, tap % 3 - 1
    out = ((dy == -1) & (y == side - 1)) | ((dy == 1) & (y == 0))
    out = out | ((dx == -1) & (x == side - 1)) | ((dx == 1) & (x == 0))
    inside = (tap == TAPS) | ((tap < TAPS) & jnp.logical_not(out))
    return jnp.where(inside, 1.0, 0.0).astype(BF)


def front_kernel(
    side,
    counts_hbm,
    dests_hbm,
    ends_hbm,
    rewards_hbm,
    ratios_hbm,
    valid_hbm,
    frames_hbm,
    stored_hbm,
    stem_hbm,
    first_hbm,
    second_hbm,
    head_hbm,
    discounts_hbm,
    lambdas_hbm,
    middle_hbm,
    hidden_hbm,
    values_ref,
    send_ref,
    chain_ref,
    loads_ref,
    frames,
    stem,
    weights,
    flat,
    hidden,
    act,
    mid,
    sums,
    kept,
    mixed,
    counts_ref,
    dests_ref,
    ends_ref,
    rewards_ref,
    ratios_ref,
    valid_ref,
    stored_ref,
    head_ref,
    discounts_ref,
    lambdas_ref,
    sems,
):
    steps = frames.shape[0]
    half = side // 2
    sem = iter(range(64))

    def load(src, dst):
        copy = pltpu.make_async_copy(src, dst, sems.at[next(sem)])
        copy.start()
        return copy

    stem_copy = load(stem_hbm, stem)
    frame_copies = [pltpu.make_async_copy(frames_hbm.at[b], frames.at[b], sems.at[next(sem)]) for b in range(steps)]
    weight_copies = [
        pltpu.make_async_copy(src, weights.at[i], sems.at[next(sem)])
        for i, src in enumerate((first_hbm.at[0], second_hbm.at[0], first_hbm.at[1], second_hbm.at[1]))
    ]
    frame_copies[0].start()
    weight_copies[0].start()
    frame_copies[1].start()
    small = [
        load(src, dst)
        for src, dst in (
            (counts_hbm, counts_ref),
            (dests_hbm, dests_ref),
            (ends_hbm, ends_ref),
            (rewards_hbm, rewards_ref),
            (ratios_hbm, ratios_ref),
            (valid_hbm, valid_ref),
            (stored_hbm, stored_ref),
            (head_hbm, head_ref),
            (discounts_hbm, discounts_ref),
            (lambdas_hbm, lambdas_ref),
        )
    ]
    hidden_copy = pltpu.make_async_copy(hidden, hidden_hbm, sems.at[next(sem)])
    middle_sem = next(sem)

    def middle_copy(b):
        return pltpu.make_async_copy(mid.at[b], middle_hbm.at[b], sems.at[middle_sem + b])

    stem_copy.wait()

    def begin(b):
        for c in range(steps):

            @pl.when(b == c)
            def _():
                frame_copies[c].wait()
                if c + 2 < steps:
                    frame_copies[c + 2].start()
                else:
                    for i in range(c - 1, 2 * c - 2):
                        weight_copies[i].start()

        rows = jnp.maximum(jnp.dot(frames[b], stem[...], preferred_element_type=F32), 0.0)
        for c in range(flat.shape[0]):
            flat[c] = rows[:, 128 * c : 128 * c + 128]
        start = tile_order(flat, side).astype(BF)
        hidden[b] = start.reshape(hidden.shape[1:])
        put_padded(act, b, normed(start), 0, half)

    def layer(l, _):
        def first(b, _):
            @pl.when(l == 0)
            def _():
                begin(b)

            @pl.when((l == 0) & (b == 0))
            def _():
                weight_copies[0].wait()
                mix_weights(weights.at[0], mixed)

            @pl.when((l == 1) & (b == 0))
            def _():
                weight_copies[2].wait()
                mix_weights(weights.at[2], mixed)

            for y0 in range(0, half, CHUNK):
                out = conv(act, b, weights.at[2 * l], mixed, y0, CHUNK)
                put_padded(mid, b, jnp.maximum(out, 0.0), y0, half)

            @pl.when(l == 1)
            def _():
                middle_copy(b).start()

            return 0

        def second(b, _):
            for y0 in range(0, half, CHUNK):
                out = conv(mid, b, weights.at[1], mixed, y0, CHUNK)
                now = hidden[b, y0 : y0 + CHUNK].astype(F32).reshape(out.shape) + out
                now = now.astype(BF)
                hidden[b, y0 : y0 + CHUNK] = now.reshape((CHUNK,) + hidden.shape[2:])
                put_padded(act, b, normed(now), y0, half)
            return 0

        lax.fori_loop(0, steps, first, 0)

        @pl.when(l == 0)
        def _():
            weight_copies[1].wait()
            mix_weights(weights.at[1], mixed)
            lax.fori_loop(0, steps, second, 0)
            hidden_copy.start()

        return 0

    lax.fori_loop(0, 2, layer, 0)

    select = window_rows(side)
    width = hidden.shape[-1]

    def total(b, _):
        block = mid[b, 1 : half + 1, 1 : mid.shape[2] - 1].reshape(side * side, width)
        rows = hidden[b].reshape(side * side, width)
        sums[b] = jnp.dot(select, block, preferred_element_type=F32)
        kept[b] = jnp.dot(select, rows, preferred_element_type=F32)
        return 0

    lax.fori_loop(0, steps, total, 0)
    weight_copies[3].wait()
    pooled = None
    for tap in range(TAPS):
        exact = jnp.concatenate([sums[b, tap : tap + 1] for b in range(steps)], axis=0)
        parts, rest = [], exact
        for _ in range(3):
            part = rest.astype(BF)
            parts.append(part.astype(F32))
            rest = rest - part.astype(F32)
        stacked = jnp.concatenate(parts + [jnp.zeros_like(exact)], axis=0).astype(BF)
        term = jnp.dot(stacked, weights[3, tap], preferred_element_type=F32)
        pooled = term if pooled is None else pooled + term
    pooled = pooled[0:steps] + pooled[steps : 2 * steps] + pooled[2 * steps : 3 * steps]
    pooled = (pooled + jnp.concatenate([kept[b, TAPS : TAPS + 1] for b in range(steps)], axis=0)) * (1.0 / (side * side))
    for copy in small:
        copy.wait()
    fresh = jnp.dot(
        pooled,
        head_ref[...].astype(F32),
        precision=lax.Precision.HIGHEST,
        preferred_element_type=F32,
    )
    discount = discounts_ref[...]
    trace = lambdas_ref[...]
    rows = []
    for t in range(steps):
        live = jnp.full((1, fresh.shape[1]), counts_ref[0, t], jnp.int32) > 0
        rows.append(jnp.where(live, fresh[t : t + 1], stored_ref[t : t + 1]))
        values_ref[t : t + 1] = rows[t]
    add = jnp.zeros_like(discount)
    mul = jnp.ones_like(discount)
    last = jnp.zeros_like(discount)
    for t in range(steps - 1, -1, -1):
        going = 1.0 - ends_ref[0, t].astype(F32)
        cut = jnp.minimum(1.0, ratios_ref[0, t])
        weight = discount * going * (1.0 - trace * cut)
        step_mul = discount * trace * cut * going
        reward = rewards_ref[0, t]
        if t == steps - 1:
            add = reward + step_mul * add
            last = weight
        else:
            add = reward + weight * rows[t + 1] + step_mul * add
            last = step_mul * last
        mul = step_mul * mul
        valid = valid_ref[0, t].astype(F32)
        chain_ref[t : t + 1] = valid * add
        chain_ref[steps + t : steps + t + 1] = valid * mul
        chain_ref[2 * steps + t : 2 * steps + t + 1] = valid * last
    shards = send_ref.shape[0]
    for place, row in enumerate((add, mul, last, rows[0])):
        send_ref[:, place : place + 1, :] = jnp.broadcast_to(row[None], (shards, 1, row.shape[1]))
    for g in range(loads_ref.shape[0]):
        load_here = jnp.int32(0)
        for t in range(steps):
            load_here = load_here + jnp.where(dests_ref[0, t] == g, jnp.maximum(counts_ref[0, t], 0), 0)
        loads_ref[g] = jnp.full((1, 128), load_here, jnp.int32)
    hidden_copy.wait()
    for b in range(steps):
        middle_copy(b).wait()


def back_kernel(side, counts_ref, middle_hbm, hidden_hbm, second_hbm, out_hbm, mid, hidden, weight, mixed, flat, done, sems):
    steps = mid.shape[0]
    half, third = side // 2, side // LANE
    copies = []

    def load(i, src, dst):
        copy = pltpu.make_async_copy(src, dst, sems.at[i])
        copy.start()
        return copy

    weight_copy = load(0, second_hbm.at[1], weight)
    for b in range(steps):
        copies.append(
            (
                load(1 + 3 * b, middle_hbm.at[b], mid.at[b]),
                load(2 + 3 * b, hidden_hbm.at[b], hidden.at[b]),
            )
        )
    weight_copy.wait()
    mix_weights(weight, mixed)

    def finish(b, _):
        pltpu.make_async_copy(middle_hbm.at[b], mid.at[b], sems.at[1 + 3 * b]).wait()
        pltpu.make_async_copy(hidden_hbm.at[b], hidden.at[b], sems.at[2 + 3 * b]).wait()
        live = counts_ref[0, b] > 0
        for y0 in range(0, half, CHUNK):
            out = conv(mid, b, weight, mixed, y0, CHUNK)
            out = hidden[b, y0 : y0 + CHUNK].astype(F32).reshape(out.shape) + out
            out = jnp.where(live, out, jnp.zeros_like(out))
            for y in range(CHUNK):
                for j in range(third):
                    for h in range(2):
                        start = side * (half * h + y0 + y) + j
                        for c in range(flat.shape[0]):
                            flat[c, pl.ds(start, LANE, stride=third), :] = out[y, j, h, :, 128 * c : 128 * c + 128]
        for c in range(flat.shape[0]):
            done[b, :, 128 * c : 128 * c + 128] = flat[c].astype(BF)
        pltpu.make_async_copy(done.at[b], out_hbm.at[b], sems.at[3 + 3 * b]).start()
        return 0

    lax.fori_loop(0, steps, finish, 0)
    for b in range(steps):
        pltpu.make_async_copy(done.at[b], out_hbm.at[b], sems.at[3 + 3 * b]).wait()


SMEM = pl.BlockSpec(memory_space=pltpu.SMEM)
VMEM = pl.BlockSpec(memory_space=pltpu.VMEM)
ANY = pl.BlockSpec(memory_space=pl.ANY)
HBM = pl.BlockSpec(memory_space=pltpu.HBM)


def front(counts, dests, ends, rewards, ratios, valid, frames, stored, stem, first, second, head, discounts, lambdas, shards, groups):
    steps, side, _, pdim = frames.shape
    width, heads = stem.shape[1], head.shape[1]
    half, third = side // 2, side // LANE
    padded = (steps, half + 2, third + 2, 2 * LANE, width)
    plain = (steps, half, third, 2 * LANE, width)
    area = side * side
    work = steps * area * 2 * width * (pdim + 3 * TAPS * width)
    return pl.pallas_call(
        functools.partial(front_kernel, side),
        out_shape=(
            jax.ShapeDtypeStruct(padded, BF),
            jax.ShapeDtypeStruct(plain, BF),
            jax.ShapeDtypeStruct((steps, heads), F32),
            jax.ShapeDtypeStruct((shards, 4, heads), F32),
            jax.ShapeDtypeStruct((3 * steps, heads), F32),
            jax.ShapeDtypeStruct((groups, 1, 128), jnp.int32),
        ),
        in_specs=[HBM] * 14,
        out_specs=(ANY, ANY, VMEM, VMEM, VMEM, VMEM),
        scratch_shapes=[
            pltpu.VMEM((steps, area, pdim), BF),
            pltpu.VMEM(stem.shape, BF),
            pltpu.VMEM((4, TAPS, width, width), BF),
            pltpu.VMEM((width // 128, area, 128), F32),
            pltpu.VMEM(plain, BF),
            pltpu.VMEM(padded, BF),
            pltpu.VMEM(padded, BF),
            pltpu.VMEM((steps, 2 * LANE, width), F32),
            pltpu.VMEM((steps, 2 * LANE, width), F32),
            pltpu.VMEM((6, width, width), BF),
            pltpu.SMEM(counts.shape, jnp.int32),
            pltpu.SMEM(dests.shape, jnp.int32),
            pltpu.SMEM(ends.shape, jnp.int32),
            pltpu.SMEM(rewards.shape, F32),
            pltpu.SMEM(ratios.shape, F32),
            pltpu.SMEM(valid.shape, jnp.int32),
            pltpu.VMEM(stored.shape, F32),
            pltpu.VMEM(head.shape, BF),
            pltpu.VMEM(discounts.shape, F32),
            pltpu.VMEM(lambdas.shape, F32),
            pltpu.SemaphoreType.DMA((32,)),
        ],
        compiler_params=pltpu.CompilerParams(vmem_limit_bytes=FRONT_GRANT),
        cost_estimate=pl.CostEstimate(flops=work, bytes_accessed=16 * 10**6, transcendentals=0),
    )(counts, dests, ends, rewards, ratios, valid, frames.reshape(steps, area, pdim), stored, stem, first, second, head, discounts, lambdas)


def back(counts, middle, hidden, second, side):
    steps, width = middle.shape[0], middle.shape[-1]
    area = side * side
    return pl.pallas_call(
        functools.partial(back_kernel, side),
        out_shape=jax.ShapeDtypeStruct((steps, area, width), BF),
        in_specs=[SMEM, ANY, ANY, HBM],
        out_specs=HBM,
        scratch_shapes=[
            pltpu.VMEM(middle.shape, BF),
            pltpu.VMEM(hidden.shape, BF),
            pltpu.VMEM((TAPS, width, width), BF),
            pltpu.VMEM((6, width, width), BF),
            pltpu.VMEM((width // 128, area, 128), F32),
            pltpu.VMEM((steps, area, width), BF),
            pltpu.SemaphoreType.DMA((32,)),
        ],
        compiler_params=pltpu.CompilerParams(vmem_limit_bytes=BACK_GRANT),
        cost_estimate=pl.CostEstimate(
            flops=steps * area * 2 * width * TAPS * width, bytes_accessed=8 * 10**6, transcendentals=0
        ),
    )(counts, middle, hidden, second)


def target_kernel(steps, loads_hbm, chain_hbm, got_hbm, targets_ref, load_ref, loads_ref, chain_ref, got_ref, sems):
    shard = lax.axis_index("tm")
    shards, width = got_ref.shape[0], chain_ref.shape[1]
    pairs = ((got_hbm, got_ref), (chain_hbm, chain_ref), (loads_hbm, loads_ref))
    copies = [pltpu.make_async_copy(src, dst, sems.at[i]) for i, (src, dst) in enumerate(pairs)]
    for copy in copies:
        copy.start()
    for copy in copies:
        copy.wait()
    zero = jnp.zeros((1, width), F32)
    carry, first = zero, zero
    kept_carry, kept_first = zero, zero
    for s in range(shards - 1, -1, -1):
        carry = got_ref[s, 0:1] + got_ref[s, 1:2] * carry + got_ref[s, 2:3] * first
        first = got_ref[s, 3:4]
        follows = jnp.full((1, width), shard + 1, jnp.int32) == s
        kept_carry = jnp.where(follows, carry, kept_carry)
        kept_first = jnp.where(follows, first, kept_first)
    for t in range(steps):
        targets_ref[t : t + 1] = (
            chain_ref[t : t + 1]
            + chain_ref[steps + t : steps + t + 1] * kept_carry
            + chain_ref[2 * steps + t : 2 * steps + t + 1] * kept_first
        )
    load = loads_ref[0]
    for g in range(1, loads_ref.shape[0]):
        load = load + loads_ref[g]
    load_ref[...] = load[:, 0:1]


def per_device(
    frames,
    sample_counts,
    dest_groups,
    episode_ends,
    valid_steps,
    rewards,
    ratios,
    stored_values,
    stem_weight,
    conv_first,
    conv_second,
    value_weight,
    discounts,
    lambdas,
):
    steps, side = frames.shape[1], frames.shape[2]
    width = stem_weight.shape[1]
    heads = value_weight.shape[1]
    groups, shards = lax.axis_size("grp"), lax.axis_size("tm")
    middle, hidden, values, send, chain, loads = front(
        sample_counts,
        dest_groups,
        episode_ends,
        rewards,
        ratios,
        valid_steps,
        frames[0],
        stored_values[0],
        stem_weight,
        conv_first,
        conv_second,
        value_weight,
        discounts[None],
        lambdas[None],
        shards,
        groups,
    )
    got = lax.all_to_all(send, "tm", split_axis=0, concat_axis=0, tiled=True)
    loads = lax.all_to_all(loads, "grp", split_axis=0, concat_axis=0, tiled=True)
    latents = back(sample_counts, middle, hidden, conv_second, side)
    targets, load = pl.pallas_call(
        functools.partial(target_kernel, steps),
        out_shape=(
            jax.ShapeDtypeStruct((steps, heads), F32),
            jax.ShapeDtypeStruct((1, 1), jnp.int32),
        ),
        in_specs=[ANY] * 3,
        out_specs=(VMEM, VMEM),
        scratch_shapes=[
            pltpu.VMEM(loads.shape, jnp.int32),
            pltpu.VMEM(chain.shape, F32),
            pltpu.VMEM(got.shape, F32),
            pltpu.SemaphoreType.DMA((3,)),
        ],
        compiler_params=pltpu.CompilerParams(vmem_limit_bytes=BACK_GRANT),
    )(loads, chain, got)
    latents = latents.reshape(1, steps, side, side, width)
    return latents, values[None], targets[None], load


def solution(mesh):
    rows = P("grp", "tm")
    deep = P("grp", "tm", None)
    whole = P("grp", "tm", None, None, None)
    in_specs = (whole,) + (rows,) * 6 + (deep,) + (P(),) * 6
    out_specs = (whole, deep, deep, rows)
    return jax.shard_map(
        per_device, mesh=mesh, in_specs=in_specs, out_specs=out_specs, check_vma=False
    )
```

```python
import functools

import jax
import jax.numpy as jnp
from jax import lax
from jax.experimental import pallas as pl
from jax.experimental.pallas import tpu as pltpu
from jax.sharding import PartitionSpec as P

BF = jnp.bfloat16
F32 = jnp.float32
LANE = 8
TAPS = 9
WINO = True
CHUNK = 12
FRONT_GRANT = 60 * 2**20
BACK_GRANT = 60 * 2**20
LAST_GRANT = 40 * 2**20
TALL = 2**16


def tile_order(flat_ref, side):
    half, third = side // 2, side // LANE
    tiles = []
    for y in range(half):
        for j in range(third):
            for h in range(2):
                start = side * (half * h + y) + j
                rows = pl.ds(start, LANE, stride=third)
                parts = [flat_ref[c, rows, :] for c in range(flat_ref.shape[0])]
                tiles.append(jnp.concatenate(parts, axis=1))
    return jnp.stack(tiles).reshape(half, third, 2, LANE, -1)


def put_padded(out_ref, b, tiles, y0, half):
    count, third, _, _, width = tiles.shape
    place = lax.broadcasted_iota(jnp.int32, (count * 2, LANE, width), 1)
    before = pltpu.roll(tiles[:, third - 1].reshape(count * 2, LANE, width), 1, 1)
    before = jnp.where(place == 0, 0.0, before).reshape(count, 1, 2, LANE, width)
    after = pltpu.roll(tiles[:, 0].reshape(count * 2, LANE, width), LANE - 1, 1)
    after = jnp.where(place == LANE - 1, 0.0, after).reshape(count, 1, 2, LANE, width)
    wide = jnp.concatenate([before, tiles, after], axis=1)
    rows = wide.reshape(count, third + 2, 2 * LANE, width).astype(BF)
    out_ref[b, y0 + 1 : y0 + count + 1] = rows
    none = jnp.zeros((third + 2, 1, LANE, width), F32)
    if y0 + count == half:
        top = jnp.concatenate([none, wide[count - 1, :, 0:1]], axis=1)
        out_ref[b, 0] = top.reshape(third + 2, 2 * LANE, width).astype(BF)
    if y0 == 0:
        bottom = jnp.concatenate([wide[0, :, 1:2], none], axis=1)
        out_ref[b, half + 1] = bottom.reshape(third + 2, 2 * LANE, width).astype(BF)


def normed(hidden):
    wide = hidden.astype(F32)
    scale = lax.rsqrt(jnp.mean(wide * wide, axis=-1, keepdims=True) + 1e-05)
    return jnp.maximum(wide * scale, 0.0)


def conv(src_ref, b, weight_ref, mixed_ref, y0, count):
    _, tall, broad, rows, width = src_ref.shape
    third = broad - 2
    if not WINO:
        total = None
        for tap in range(TAPS):
            dy, dx = tap // 3, tap % 3
            window = src_ref[b, y0 + dy : y0 + dy + count, dx : dx + third].reshape(count * third * rows, width)
            part = jnp.dot(window, weight_ref[tap], preferred_element_type=F32)
            total = part if total is None else total + part
        return total.reshape(count, third, 2, LANE, weight_ref.shape[2])
    pairs = count // 2
    block = src_ref[b, y0 : y0 + count + 2].reshape(pairs + 1, 2, broad, rows, width)
    e0, e1, e2, e3 = block[:pairs, 0], block[:pairs, 1], block[1:, 0], block[1:, 1]
    parts = []
    for k, mix in enumerate((e0 - e2, e1 + e2, e2 - e1, e1 - e3)):
        total = None
        for dx in range(3):
            weight = (weight_ref[dx], mixed_ref[dx], mixed_ref[3 + dx], weight_ref[6 + dx])[k]
            window = mix[:, dx : dx + third].reshape(pairs * third * rows, width)
            part = jnp.dot(window, weight, preferred_element_type=F32)
            total = part if total is None else total + part
        parts.append(total)
    low = parts[0] + parts[1] + parts[2]
    high = parts[1] - parts[2] - parts[3]
    out = jnp.stack([x.reshape(pairs, third, 2, LANE, -1) for x in (low, high)], axis=1)
    return out.reshape(count, third, 2, LANE, -1)


def mix_weights(weight_ref, mixed_ref):
    if not WINO:
        return
    size = weight_ref.shape[1]

    def some(i, _):
        rows = pl.ds(pl.multiple_of(i * 64, 64), 64)
        for dx in range(3):
            outer = weight_ref[dx, rows].astype(F32) + weight_ref[6 + dx, rows].astype(F32)
            inner = weight_ref[3 + dx, rows].astype(F32)
            mixed_ref[dx, rows] = (0.5 * (outer + inner)).astype(BF)
            mixed_ref[3 + dx, rows] = (0.5 * (outer - inner)).astype(BF)
        return 0

    lax.fori_loop(0, size // 64, some, 0)


def window_rows(side):
    half, third = side // 2, side // LANE
    shape = (2 * LANE, side * side)
    tap = lax.broadcasted_iota(jnp.int32, shape, 0)
    at = lax.broadcasted_iota(jnp.int32, shape, 1)
    s = at % LANE
    h = (at // LANE) % 2
    j = (at // (2 * LANE)) % third
    y = at // (2 * LANE * third) + half * h
    x = s * third + j
    dy, dx = tap // 3 - 1, tap % 3 - 1
    out = ((dy == -1) & (y == side - 1)) | ((dy == 1) & (y == 0))
    out = out | ((dx == -1) & (x == side - 1)) | ((dx == 1) & (x == 0))
    inside = (tap == TAPS) | ((tap < TAPS) & jnp.logical_not(out))
    return jnp.where(inside, 1.0, 0.0).astype(BF)


def front_kernel(
    side,
    counts_hbm,
    ends_hbm,
    rewards_hbm,
    ratios_hbm,
    valid_hbm,
    frames_hbm,
    stored_hbm,
    stem_hbm,
    first_hbm,
    second_hbm,
    head_hbm,
    discounts_hbm,
    lambdas_hbm,
    middle_hbm,
    hidden_hbm,
    values_ref,
    send_ref,
    chain_hbm,
    frames,
    stem,
    weights,
    flat,
    hidden,
    act,
    mid,
    sums,
    kept,
    mixed,
    chain_ref,
    counts_ref,
    ends_ref,
    rewards_ref,
    ratios_ref,
    valid_ref,
    stored_ref,
    head_ref,
    discounts_ref,
    lambdas_ref,
    sems,
):
    steps = frames.shape[0]
    half = side // 2
    sem = iter(range(64))

    def load(src, dst):
        copy = pltpu.make_async_copy(src, dst, sems.at[next(sem)])
        copy.start()
        return copy

    stem_copy = load(stem_hbm, stem)
    frame_copies = [pltpu.make_async_copy(frames_hbm.at[b], frames.at[b], sems.at[next(sem)]) for b in range(steps)]
    weight_copies = [
        pltpu.make_async_copy(src, weights.at[i], sems.at[next(sem)])
        for i, src in enumerate((first_hbm.at[0], second_hbm.at[0], first_hbm.at[1], second_hbm.at[1]))
    ]
    frame_copies[0].start()
    weight_copies[0].start()
    frame_copies[1].start()
    small = [
        load(src, dst)
        for src, dst in (
            (counts_hbm, counts_ref),
            (ends_hbm, ends_ref),
            (rewards_hbm, rewards_ref),
            (ratios_hbm, ratios_ref),
            (valid_hbm, valid_ref),
            (stored_hbm, stored_ref),
            (head_hbm, head_ref),
            (discounts_hbm, discounts_ref),
            (lambdas_hbm, lambdas_ref),
        )
    ]
    hidden_copy = pltpu.make_async_copy(hidden, hidden_hbm, sems.at[next(sem)])
    middle_sem = 24

    def middle_copy(b):
        return pltpu.make_async_copy(mid.at[b], middle_hbm.at[b], sems.at[middle_sem + b])

    stem_copy.wait()

    def begin(b):
        for c in range(steps):

            @pl.when(b == c)
            def _():
                frame_copies[c].wait()
                if c + 2 < steps:
                    frame_copies[c + 2].start()
                else:
                    for i in range(c - 1, 2 * c - 2):
                        weight_copies[i].start()

        rows = jnp.maximum(jnp.dot(frames[b], stem[...], preferred_element_type=F32), 0.0)
        for c in range(flat.shape[0]):
            flat[c] = rows[:, 128 * c : 128 * c + 128]
        start = tile_order(flat, side).astype(BF)
        hidden[b] = start.reshape(hidden.shape[1:])
        put_padded(act, b, normed(start), 0, half)

    def layer(l, _):
        def first(b, _):
            @pl.when(l == 0)
            def _():
                begin(b)

            @pl.when((l == 0) & (b == 0))
            def _():
                weight_copies[0].wait()
                mix_weights(weights.at[0], mixed)

            @pl.when((l == 1) & (b == 0))
            def _():
                weight_copies[2].wait()
                mix_weights(weights.at[2], mixed)

            for y0 in range(0, half, CHUNK):
                out = conv(act, b, weights.at[2 * l], mixed, y0, CHUNK)
                put_padded(mid, b, jnp.maximum(out, 0.0), y0, half)

            @pl.when(l == 1)
            def _():
                middle_copy(b).start()

            return 0

        def second(b, _):
            for y0 in range(0, half, CHUNK):
                out = conv(mid, b, weights.at[1], mixed, y0, CHUNK)
                now = hidden[b, y0 : y0 + CHUNK].astype(F32).reshape(out.shape) + out
                now = now.astype(BF)
                hidden[b, y0 : y0 + CHUNK] = now.reshape((CHUNK,) + hidden.shape[2:])
                put_padded(act, b, normed(now), y0, half)
            return 0

        lax.fori_loop(0, steps, first, 0)

        @pl.when(l == 0)
        def _():
            weight_copies[1].wait()
            mix_weights(weights.at[1], mixed)
            lax.fori_loop(0, steps, second, 0)
            hidden_copy.start()

        return 0

    lax.fori_loop(0, 2, layer, 0)

    select = window_rows(side)
    width = hidden.shape[-1]

    def total(b, _):
        block = mid[b, 1 : half + 1, 1 : mid.shape[2] - 1].reshape(side * side, width)
        rows = hidden[b].reshape(side * side, width)
        sums[b] = jnp.dot(select, block, preferred_element_type=F32)
        kept[b] = jnp.dot(select, rows, preferred_element_type=F32)
        return 0

    lax.fori_loop(0, steps, total, 0)
    weight_copies[3].wait()
    pooled = None
    for tap in range(TAPS):
        exact = jnp.concatenate([sums[b, tap : tap + 1] for b in range(steps)], axis=0)
        parts, rest = [], exact
        for _ in range(3):
            part = rest.astype(BF)
            parts.append(part.astype(F32))
            rest = rest - part.astype(F32)
        stacked = jnp.concatenate(parts + [jnp.zeros_like(exact)], axis=0).astype(BF)
        term = jnp.dot(stacked, weights[3, tap], preferred_element_type=F32)
        pooled = term if pooled is None else pooled + term
    pooled = pooled[0:steps] + pooled[steps : 2 * steps] + pooled[2 * steps : 3 * steps]
    pooled = (pooled + jnp.concatenate([kept[b, TAPS : TAPS + 1] for b in range(steps)], axis=0)) * (1.0 / (side * side))
    for copy in small:
        copy.wait()
    fresh = jnp.dot(
        pooled,
        head_ref[...].astype(F32),
        precision=lax.Precision.HIGHEST,
        preferred_element_type=F32,
    )
    discount = discounts_ref[...]
    trace = lambdas_ref[...]
    rows = []
    for t in range(steps):
        live = jnp.full((1, fresh.shape[1]), counts_ref[0, t], jnp.int32) > 0
        rows.append(jnp.where(live, fresh[t : t + 1], stored_ref[t : t + 1]))
        values_ref[t : t + 1] = rows[t]
    add = jnp.zeros_like(discount)
    mul = jnp.ones_like(discount)
    last = jnp.zeros_like(discount)
    for t in range(steps - 1, -1, -1):
        going = 1.0 - ends_ref[0, t].astype(F32)
        cut = jnp.minimum(1.0, ratios_ref[0, t])
        weight = discount * going * (1.0 - trace * cut)
        step_mul = discount * trace * cut * going
        reward = rewards_ref[0, t]
        if t == steps - 1:
            add = reward + step_mul * add
            last = weight
        else:
            add = reward + weight * rows[t + 1] + step_mul * add
            last = step_mul * last
        mul = step_mul * mul
        valid = valid_ref[0, t].astype(F32)
        chain_ref[t : t + 1] = valid * add
        chain_ref[steps + t : steps + t + 1] = valid * mul
        chain_ref[2 * steps + t : 2 * steps + t + 1] = valid * last
    chain_copy = load(chain_ref, chain_hbm.at[pl.ds(0, 3 * steps)])
    shards = send_ref.shape[0]
    for place, row in enumerate((add, mul, last, rows[0])):
        send_ref[:, place : place + 1, :] = jnp.broadcast_to(row[None], (shards, 1, row.shape[1]))
    chain_copy.wait()
    hidden_copy.wait()
    for b in range(steps):
        middle_copy(b).wait()


def back_kernel(side, groups, *refs):
    routed = refs[:groups]
    middle_hbm, hidden_hbm, second_hbm, out_hbm, load_ref = refs[groups : groups + 5]
    held = refs[groups + 5 : 2 * groups + 5]
    mid, hidden, weight, mixed, flat, done, sems = refs[2 * groups + 5 :]
    steps = mid.shape[0]
    small = [pltpu.make_async_copy(src, dst, sems.at[16 + i]) for i, (src, dst) in enumerate(zip(routed, held))]
    for copy in small:
        copy.start()
    half, third = side // 2, side // LANE
    copies = []

    def load(i, src, dst):
        copy = pltpu.make_async_copy(src, dst, sems.at[i])
        copy.start()
        return copy

    weight_copy = load(0, second_hbm.at[1], weight)
    for b in range(steps):
        copies.append(
            (
                load(1 + 3 * b, middle_hbm.at[b], mid.at[b]),
                load(2 + 3 * b, hidden_hbm.at[b], hidden.at[b]),
            )
        )
    for copy in small:
        copy.wait()
    weight_copy.wait()
    mix_weights(weight, mixed)

    def finish(b, _):
        pltpu.make_async_copy(middle_hbm.at[b], mid.at[b], sems.at[1 + 3 * b]).wait()
        pltpu.make_async_copy(hidden_hbm.at[b], hidden.at[b], sems.at[2 + 3 * b]).wait()
        live = held[0][0, b] >= groups
        for y0 in range(0, half, CHUNK):
            out = conv(mid, b, weight, mixed, y0, CHUNK)
            out = hidden[b, y0 : y0 + CHUNK].astype(F32).reshape(out.shape) + out
            out = jnp.where(live, out, jnp.zeros_like(out))
            for y in range(CHUNK):
                for j in range(third):
                    for h in range(2):
                        start = side * (half * h + y0 + y) + j
                        for c in range(flat.shape[0]):
                            flat[c, pl.ds(start, LANE, stride=third), :] = out[y, j, h, :, 128 * c : 128 * c + 128]
        for c in range(flat.shape[0]):
            done[b, :, 128 * c : 128 * c + 128] = flat[c].astype(BF)
        pltpu.make_async_copy(done.at[b], out_hbm.at[b], sems.at[3 + 3 * b]).start()
        return 0

    lax.fori_loop(0, steps, finish, 0)
    group = lax.axis_index("grp")
    total = jnp.int32(0)
    for codes in held:
        for t in range(steps):
            code = codes[0, t]
            total = total + jnp.where(code % groups == group, code // groups, 0)
    load_ref[0, 0] = total
    for b in range(steps):
        pltpu.make_async_copy(done.at[b], out_hbm.at[b], sems.at[3 + 3 * b]).wait()


SMEM = pl.BlockSpec(memory_space=pltpu.SMEM)
VMEM = pl.BlockSpec(memory_space=pltpu.VMEM)
ANY = pl.BlockSpec(memory_space=pl.ANY)
HBM = pl.BlockSpec(memory_space=pltpu.HBM)


def front(counts, ends, rewards, ratios, valid, frames, stored, stem, first, second, head, discounts, lambdas, shards):
    steps, side, _, pdim = frames.shape
    width, heads = stem.shape[1], head.shape[1]
    half, third = side // 2, side // LANE
    padded = (steps, half + 2, third + 2, 2 * LANE, width)
    plain = (steps, half, third, 2 * LANE, width)
    area = side * side
    work = steps * area * 2 * width * (pdim + 3 * TAPS * width)
    return pl.pallas_call(
        functools.partial(front_kernel, side),
        out_shape=(
            jax.ShapeDtypeStruct(padded, BF),
            jax.ShapeDtypeStruct(plain, BF),
            jax.ShapeDtypeStruct((steps, heads), F32),
            jax.ShapeDtypeStruct((shards, 4, heads), F32),
            jax.ShapeDtypeStruct((TALL, heads), F32),
        ),
        in_specs=[HBM] * 13,
        out_specs=(ANY, ANY, VMEM, VMEM, ANY),
        scratch_shapes=[
            pltpu.VMEM((steps, area, pdim), BF),
            pltpu.VMEM(stem.shape, BF),
            pltpu.VMEM((4, TAPS, width, width), BF),
            pltpu.VMEM((width // 128, area, 128), F32),
            pltpu.VMEM(plain, BF),
            pltpu.VMEM(padded, BF),
            pltpu.VMEM(padded, BF),
            pltpu.VMEM((steps, 2 * LANE, width), F32),
            pltpu.VMEM((steps, 2 * LANE, width), F32),
            pltpu.VMEM((6, width, width), BF),
            pltpu.VMEM((3 * steps, heads), F32),
            pltpu.SMEM(counts.shape, jnp.int32),
            pltpu.SMEM(ends.shape, jnp.int32),
            pltpu.SMEM(rewards.shape, F32),
            pltpu.SMEM(ratios.shape, F32),
            pltpu.SMEM(valid.shape, jnp.int32),
            pltpu.VMEM(stored.shape, F32),
            pltpu.VMEM(head.shape, BF),
            pltpu.VMEM(discounts.shape, F32),
            pltpu.VMEM(lambdas.shape, F32),
            pltpu.SemaphoreType.DMA((32,)),
        ],
        compiler_params=pltpu.CompilerParams(vmem_limit_bytes=FRONT_GRANT),
        cost_estimate=pl.CostEstimate(flops=work, bytes_accessed=16 * 10**6, transcendentals=0),
    )(counts, ends, rewards, ratios, valid, frames.reshape(steps, area, pdim), stored, stem, first, second, head, discounts, lambdas)


def back(routed, middle, hidden, second, side):
    steps, width = middle.shape[0], middle.shape[-1]
    area = side * side
    return pl.pallas_call(
        functools.partial(back_kernel, side, len(routed)),
        out_shape=(
            jax.ShapeDtypeStruct((steps, area, width), BF),
            jax.ShapeDtypeStruct((1, 1), jnp.int32),
        ),
        in_specs=[ANY] * len(routed) + [ANY, ANY, HBM],
        out_specs=(HBM, SMEM),
        scratch_shapes=[pltpu.SMEM(routed[0].shape, jnp.int32)] * len(routed)
        + [
            pltpu.VMEM(middle.shape, BF),
            pltpu.VMEM(hidden.shape, BF),
            pltpu.VMEM((TAPS, width, width), BF),
            pltpu.VMEM((6, width, width), BF),
            pltpu.VMEM((width // 128, area, 128), F32),
            pltpu.VMEM((steps, area, width), BF),
            pltpu.SemaphoreType.DMA((32,)),
        ],
        compiler_params=pltpu.CompilerParams(vmem_limit_bytes=BACK_GRANT),
        cost_estimate=pl.CostEstimate(
            flops=steps * area * 2 * width * TAPS * width, bytes_accessed=8 * 10**6, transcendentals=0
        ),
    )(*routed, middle, hidden, second)


def target_kernel(steps, chain_hbm, got_hbm, targets_ref, chain_ref, got_ref, sems):
    shard = lax.axis_index("tm")
    shards, width = got_ref.shape[0], chain_ref.shape[1]
    pairs = ((got_hbm, got_ref), (chain_hbm.at[pl.ds(0, 3 * steps)], chain_ref))
    copies = [pltpu.make_async_copy(src, dst, sems.at[i]) for i, (src, dst) in enumerate(pairs)]
    for copy in copies:
        copy.start()
    for copy in copies:
        copy.wait()
    zero = jnp.zeros((1, width), F32)
    carry, first = zero, zero
    kept_carry, kept_first = zero, zero
    for s in range(shards - 1, -1, -1):
        carry = got_ref[s, 0:1] + got_ref[s, 1:2] * carry + got_ref[s, 2:3] * first
        first = got_ref[s, 3:4]
        follows = jnp.full((1, width), shard + 1, jnp.int32) == s
        kept_carry = jnp.where(follows, carry, kept_carry)
        kept_first = jnp.where(follows, first, kept_first)
    for t in range(steps):
        targets_ref[t : t + 1] = (
            chain_ref[t : t + 1]
            + chain_ref[steps + t : steps + t + 1] * kept_carry
            + chain_ref[2 * steps + t : 2 * steps + t + 1] * kept_first
        )

def per_device(
    frames,
    sample_counts,
    dest_groups,
    episode_ends,
    valid_steps,
    rewards,
    ratios,
    stored_values,
    stem_weight,
    conv_first,
    conv_second,
    value_weight,
    discounts,
    lambdas,
):
    steps, side = frames.shape[1], frames.shape[2]
    width = stem_weight.shape[1]
    heads = value_weight.shape[1]
    groups, shards = lax.axis_size("grp"), lax.axis_size("tm")
    codes = sample_counts * groups + dest_groups
    routed = [codes]
    for far in range(1, groups):
        routed.append(lax.ppermute(codes, "grp", [(g, (g + far) % groups) for g in range(groups)]))
    middle, hidden, values, send, chain = front(
        sample_counts,
        episode_ends,
        rewards,
        ratios,
        valid_steps,
        frames[0],
        stored_values[0],
        stem_weight,
        conv_first,
        conv_second,
        value_weight,
        discounts[None],
        lambdas[None],
        shards,
    )
    got = lax.all_to_all(send, "tm", split_axis=0, concat_axis=0, tiled=True)
    latents, load = back(routed, middle, hidden, conv_second, side)
    targets = pl.pallas_call(
        functools.partial(target_kernel, steps),
        out_shape=jax.ShapeDtypeStruct((steps, heads), F32),
        in_specs=[ANY] * 2,
        out_specs=VMEM,
        scratch_shapes=[
            pltpu.VMEM((3 * steps, heads), F32),
            pltpu.VMEM(got.shape, F32),
            pltpu.SemaphoreType.DMA((2,)),
        ],
        compiler_params=pltpu.CompilerParams(vmem_limit_bytes=LAST_GRANT),
    )(chain, got)
    latents = latents.reshape(1, steps, side, side, width)
    return latents, values[None], targets[None], load


def solution(mesh):
    rows = P("grp", "tm")
    deep = P("grp", "tm", None)
    whole = P("grp", "tm", None, None, None)
    in_specs = (whole,) + (rows,) * 6 + (deep,) + (P(),) * 6
    out_specs = (whole, deep, deep, rows)
    return jax.shard_map(
        per_device, mesh=mesh, in_specs=in_specs, out_specs=out_specs, check_vma=False
    )
```

```python
import functools

import jax
import jax.numpy as jnp
from jax import lax
from jax.experimental import pallas as pl
from jax.experimental.pallas import tpu as pltpu
from jax.sharding import PartitionSpec as P

BF = jnp.bfloat16
F32 = jnp.float32
LANE = 8
TAPS = 9
WINO = True
CHUNK = 12
FRONT_GRANT = 60 * 2**20
BACK_GRANT = 60 * 2**20
LAST_GRANT = 40 * 2**20
TALL = 2**16


def tile_order(flat_ref, side):
    half, third = side // 2, side // LANE
    tiles = []
    for y in range(half):
        for j in range(third):
            for h in range(2):
                start = side * (half * h + y) + j
                rows = pl.ds(start, LANE, stride=third)
                parts = [flat_ref[c, rows, :] for c in range(flat_ref.shape[0])]
                tiles.append(jnp.concatenate(parts, axis=1))
    return jnp.stack(tiles).reshape(half, third, 2, LANE, -1)


def put_padded(out_ref, b, tiles, y0, half):
    count, third, _, _, width = tiles.shape
    place = lax.broadcasted_iota(jnp.int32, (count * 2, LANE, width), 1)
    before = pltpu.roll(tiles[:, third - 1].reshape(count * 2, LANE, width), 1, 1)
    before = jnp.where(place == 0, 0.0, before).reshape(count, 1, 2, LANE, width)
    after = pltpu.roll(tiles[:, 0].reshape(count * 2, LANE, width), LANE - 1, 1)
    after = jnp.where(place == LANE - 1, 0.0, after).reshape(count, 1, 2, LANE, width)
    wide = jnp.concatenate([before, tiles, after], axis=1)
    rows = wide.reshape(count, third + 2, 2 * LANE, width).astype(BF)
    out_ref[b, y0 + 1 : y0 + count + 1] = rows
    none = jnp.zeros((third + 2, 1, LANE, width), F32)
    if y0 + count == half:
        top = jnp.concatenate([none, wide[count - 1, :, 0:1]], axis=1)
        out_ref[b, 0] = top.reshape(third + 2, 2 * LANE, width).astype(BF)
    if y0 == 0:
        bottom = jnp.concatenate([wide[0, :, 1:2], none], axis=1)
        out_ref[b, half + 1] = bottom.reshape(third + 2, 2 * LANE, width).astype(BF)


def normed(hidden):
    wide = hidden.astype(F32)
    scale = lax.rsqrt(jnp.mean(wide * wide, axis=-1, keepdims=True) + 1e-05)
    return jnp.maximum(wide * scale, 0.0)


def conv(src_ref, b, weight_ref, mixed_ref, y0, count):
    _, tall, broad, rows, width = src_ref.shape
    third = broad - 2
    if not WINO:
        total = None
        for tap in range(TAPS):
            dy, dx = tap // 3, tap % 3
            window = src_ref[b, y0 + dy : y0 + dy + count, dx : dx + third].reshape(count * third * rows, width)
            part = jnp.dot(window, weight_ref[tap], preferred_element_type=F32)
            total = part if total is None else total + part
        return total.reshape(count, third, 2, LANE, weight_ref.shape[2])
    pairs = count // 2
    block = src_ref[b, y0 : y0 + count + 2].reshape(pairs + 1, 2, broad, rows, width)
    e0, e1, e2, e3 = block[:pairs, 0], block[:pairs, 1], block[1:, 0], block[1:, 1]
    parts = []
    for k, mix in enumerate((e0 - e2, e1 + e2, e2 - e1, e1 - e3)):
        total = None
        for dx in range(3):
            weight = (weight_ref[dx], mixed_ref[dx], mixed_ref[3 + dx], weight_ref[6 + dx])[k]
            window = mix[:, dx : dx + third].reshape(pairs * third * rows, width)
            part = jnp.dot(window, weight, preferred_element_type=F32)
            total = part if total is None else total + part
        parts.append(total)
    low = parts[0] + parts[1] + parts[2]
    high = parts[1] - parts[2] - parts[3]
    out = jnp.stack([x.reshape(pairs, third, 2, LANE, -1) for x in (low, high)], axis=1)
    return out.reshape(count, third, 2, LANE, -1)


def mix_weights(weight_ref, mixed_ref):
    if not WINO:
        return
    size = weight_ref.shape[1]

    def some(i, _):
        rows = pl.ds(pl.multiple_of(i * 64, 64), 64)
        for dx in range(3):
            outer = weight_ref[dx, rows].astype(F32) + weight_ref[6 + dx, rows].astype(F32)
            inner = weight_ref[3 + dx, rows].astype(F32)
            mixed_ref[dx, rows] = (0.5 * (outer + inner)).astype(BF)
            mixed_ref[3 + dx, rows] = (0.5 * (outer - inner)).astype(BF)
        return 0

    lax.fori_loop(0, size // 64, some, 0)


def window_rows(side):
    half, third = side // 2, side // LANE
    shape = (2 * LANE, side * side)
    tap = lax.broadcasted_iota(jnp.int32, shape, 0)
    at = lax.broadcasted_iota(jnp.int32, shape, 1)
    s = at % LANE
    h = (at // LANE) % 2
    j = (at // (2 * LANE)) % third
    y = at // (2 * LANE * third) + half * h
    x = s * third + j
    dy, dx = tap // 3 - 1, tap % 3 - 1
    out = ((dy == -1) & (y == side - 1)) | ((dy == 1) & (y == 0))
    out = out | ((dx == -1) & (x == side - 1)) | ((dx == 1) & (x == 0))
    inside = (tap == TAPS) | ((tap < TAPS) & jnp.logical_not(out))
    return jnp.where(inside, 1.0, 0.0).astype(BF)


def front_kernel(
    side,
    counts_hbm,
    ends_hbm,
    rewards_hbm,
    ratios_hbm,
    valid_hbm,
    frames_hbm,
    stored_hbm,
    stem_hbm,
    first_hbm,
    second_hbm,
    head_hbm,
    discounts_hbm,
    lambdas_hbm,
    middle_hbm,
    hidden_hbm,
    values_ref,
    send_ref,
    chain_hbm,
    frames,
    stem,
    weights,
    flat,
    hidden,
    act,
    mid,
    sums,
    kept,
    mixed,
    chain_ref,
    counts_ref,
    ends_ref,
    rewards_ref,
    ratios_ref,
    valid_ref,
    stored_ref,
    head_ref,
    discounts_ref,
    lambdas_ref,
    sems,
):
    steps = frames.shape[0]
    half = side // 2
    sem = iter(range(64))

    def load(src, dst):
        copy = pltpu.make_async_copy(src, dst, sems.at[next(sem)])
        copy.start()
        return copy

    stem_copy = load(stem_hbm, stem)
    frame_copies = [pltpu.make_async_copy(frames_hbm.at[b], frames.at[b], sems.at[next(sem)]) for b in range(steps)]
    weight_copies = [
        pltpu.make_async_copy(src, weights.at[i], sems.at[next(sem)])
        for i, src in enumerate((first_hbm.at[0], second_hbm.at[0], first_hbm.at[1], second_hbm.at[1]))
    ]
    frame_copies[0].start()
    weight_copies[0].start()
    frame_copies[1].start()
    small = [
        load(src, dst)
        for src, dst in (
            (counts_hbm, counts_ref),
            (ends_hbm, ends_ref),
            (rewards_hbm, rewards_ref),
            (ratios_hbm, ratios_ref),
            (valid_hbm, valid_ref),
            (stored_hbm, stored_ref),
            (head_hbm, head_ref),
            (discounts_hbm, discounts_ref),
            (lambdas_hbm, lambdas_ref),
        )
    ]
    hidden_copy = pltpu.make_async_copy(hidden, hidden_hbm, sems.at[next(sem)])
    middle_sem = 24

    def middle_copy(b):
        return pltpu.make_async_copy(mid.at[b], middle_hbm.at[b], sems.at[middle_sem + b])

    stem_copy.wait()

    def begin(b):
        for c in range(steps):

            @pl.when(b == c)
            def _():
                frame_copies[c].wait()
                if c + 2 < steps:
                    frame_copies[c + 2].start()
                else:
                    for i in range(c - 1, 2 * c - 2):
                        weight_copies[i].start()

        rows = jnp.maximum(jnp.dot(frames[b], stem[...], preferred_element_type=F32), 0.0)
        for c in range(flat.shape[0]):
            flat[c] = rows[:, 128 * c : 128 * c + 128]
        start = tile_order(flat, side).astype(BF)
        hidden[b] = start.reshape(hidden.shape[1:])
        put_padded(act, b, normed(start), 0, half)

    def layer(l, _):
        def first(b, _):
            @pl.when(l == 0)
            def _():
                begin(b)

            @pl.when((l == 0) & (b == 0))
            def _():
                weight_copies[0].wait()
                mix_weights(weights.at[0], mixed)

            @pl.when((l == 1) & (b == 0))
            def _():
                weight_copies[2].wait()
                mix_weights(weights.at[2], mixed)

            for y0 in range(0, half, CHUNK):
                out = conv(act, b, weights.at[2 * l], mixed, y0, CHUNK)
                put_padded(mid, b, jnp.maximum(out, 0.0), y0, half)

            @pl.when(l == 1)
            def _():
                middle_copy(b).start()

            return 0

        def second(b, _):
            for y0 in range(0, half, CHUNK):
                out = conv(mid, b, weights.at[1], mixed, y0, CHUNK)
                now = hidden[b, y0 : y0 + CHUNK].astype(F32).reshape(out.shape) + out
                now = now.astype(BF)
                hidden[b, y0 : y0 + CHUNK] = now.reshape((CHUNK,) + hidden.shape[2:])
                put_padded(act, b, normed(now), y0, half)
            return 0

        lax.fori_loop(0, steps, first, 0)

        @pl.when(l == 0)
        def _():
            weight_copies[1].wait()
            mix_weights(weights.at[1], mixed)
            lax.fori_loop(0, steps, second, 0, unroll=2)
            hidden_copy.start()

        return 0

    lax.fori_loop(0, 2, layer, 0)

    select = window_rows(side)
    width = hidden.shape[-1]

    def total(b, _):
        block = mid[b, 1 : half + 1, 1 : mid.shape[2] - 1].reshape(side * side, width)
        rows = hidden[b].reshape(side * side, width)
        sums[b] = jnp.dot(select, block, preferred_element_type=F32)
        kept[b] = jnp.dot(select, rows, preferred_element_type=F32)
        return 0

    lax.fori_loop(0, steps, total, 0)
    weight_copies[3].wait()
    pooled = None
    for tap in range(TAPS):
        exact = jnp.concatenate([sums[b, tap : tap + 1] for b in range(steps)], axis=0)
        parts, rest = [], exact
        for _ in range(3):
            part = rest.astype(BF)
            parts.append(part.astype(F32))
            rest = rest - part.astype(F32)
        stacked = jnp.concatenate(parts + [jnp.zeros_like(exact)], axis=0).astype(BF)
        term = jnp.dot(stacked, weights[3, tap], preferred_element_type=F32)
        pooled = term if pooled is None else pooled + term
    pooled = pooled[0:steps] + pooled[steps : 2 * steps] + pooled[2 * steps : 3 * steps]
    pooled = (pooled + jnp.concatenate([kept[b, TAPS : TAPS + 1] for b in range(steps)], axis=0)) * (1.0 / (side * side))
    for copy in small:
        copy.wait()
    fresh = jnp.dot(
        pooled,
        head_ref[...].astype(F32),
        precision=lax.Precision.HIGHEST,
        preferred_element_type=F32,
    )
    discount = discounts_ref[...]
    trace = lambdas_ref[...]
    rows = []
    for t in range(steps):
        live = jnp.full((1, fresh.shape[1]), counts_ref[0, t], jnp.int32) > 0
        rows.append(jnp.where(live, fresh[t : t + 1], stored_ref[t : t + 1]))
        values_ref[t : t + 1] = rows[t]
    add = jnp.zeros_like(discount)
    mul = jnp.ones_like(discount)
    last = jnp.zeros_like(discount)
    for t in range(steps - 1, -1, -1):
        going = 1.0 - ends_ref[0, t].astype(F32)
        cut = jnp.minimum(1.0, ratios_ref[0, t])
        weight = discount * going * (1.0 - trace * cut)
        step_mul = discount * trace * cut * going
        reward = rewards_ref[0, t]
        if t == steps - 1:
            add = reward + step_mul * add
            last = weight
        else:
            add = reward + weight * rows[t + 1] + step_mul * add
            last = step_mul * last
        mul = step_mul * mul
        valid = valid_ref[0, t].astype(F32)
        chain_ref[t : t + 1] = valid * add
        chain_ref[steps + t : steps + t + 1] = valid * mul
        chain_ref[2 * steps + t : 2 * steps + t + 1] = valid * last
    chain_copy = load(chain_ref, chain_hbm.at[pl.ds(0, 3 * steps)])
    shards = send_ref.shape[0]
    for place, row in enumerate((add, mul, last, rows[0])):
        send_ref[:, place : place + 1, :] = jnp.broadcast_to(row[None], (shards, 1, row.shape[1]))
    chain_copy.wait()
    hidden_copy.wait()
    for b in range(steps):
        middle_copy(b).wait()


def back_kernel(
    side, counts_hbm, middle_hbm, hidden_hbm, second_hbm, out_hbm, counts_ref, mid, hidden, weight, mixed, flat, done, sems
):
    steps = mid.shape[0]
    counts_copy = pltpu.make_async_copy(counts_hbm, counts_ref, sems.at[16])
    counts_copy.start()
    half, third = side // 2, side // LANE
    copies = []

    def load(i, src, dst):
        copy = pltpu.make_async_copy(src, dst, sems.at[i])
        copy.start()
        return copy

    weight_copy = load(0, second_hbm.at[1], weight)
    for b in range(steps):
        copies.append(
            (
                load(1 + 3 * b, middle_hbm.at[b], mid.at[b]),
                load(2 + 3 * b, hidden_hbm.at[b], hidden.at[b]),
            )
        )
    counts_copy.wait()
    weight_copy.wait()
    mix_weights(weight, mixed)

    def finish(b, _):
        pltpu.make_async_copy(middle_hbm.at[b], mid.at[b], sems.at[1 + 3 * b]).wait()
        pltpu.make_async_copy(hidden_hbm.at[b], hidden.at[b], sems.at[2 + 3 * b]).wait()
        live = counts_ref[0, b] > 0
        for y0 in range(0, half, CHUNK):
            out = conv(mid, b, weight, mixed, y0, CHUNK)
            out = hidden[b, y0 : y0 + CHUNK].astype(F32).reshape(out.shape) + out
            out = jnp.where(live, out, jnp.zeros_like(out))
            for y in range(CHUNK):
                for j in range(third):
                    for h in range(2):
                        start = side * (half * h + y0 + y) + j
                        for c in range(flat.shape[0]):
                            flat[c, pl.ds(start, LANE, stride=third), :] = out[y, j, h, :, 128 * c : 128 * c + 128]
        for c in range(flat.shape[0]):
            done[b, :, 128 * c : 128 * c + 128] = flat[c].astype(BF)
        pltpu.make_async_copy(done.at[b], out_hbm.at[b], sems.at[3 + 3 * b]).start()
        return 0

    lax.fori_loop(0, steps, finish, 0)
    for b in range(steps):
        pltpu.make_async_copy(done.at[b], out_hbm.at[b], sems.at[3 + 3 * b]).wait()


SMEM = pl.BlockSpec(memory_space=pltpu.SMEM)
VMEM = pl.BlockSpec(memory_space=pltpu.VMEM)
ANY = pl.BlockSpec(memory_space=pl.ANY)
HBM = pl.BlockSpec(memory_space=pltpu.HBM)


def front(counts, ends, rewards, ratios, valid, frames, stored, stem, first, second, head, discounts, lambdas, shards):
    steps, side, _, pdim = frames.shape
    width, heads = stem.shape[1], head.shape[1]
    half, third = side // 2, side // LANE
    padded = (steps, half + 2, third + 2, 2 * LANE, width)
    plain = (steps, half, third, 2 * LANE, width)
    area = side * side
    work = steps * area * 2 * width * (pdim + 3 * TAPS * width)
    return pl.pallas_call(
        functools.partial(front_kernel, side),
        out_shape=(
            jax.ShapeDtypeStruct(padded, BF),
            jax.ShapeDtypeStruct(plain, BF),
            jax.ShapeDtypeStruct((steps, heads), F32),
            jax.ShapeDtypeStruct((shards, 4, heads), F32),
            jax.ShapeDtypeStruct((TALL, heads), F32),
        ),
        in_specs=[HBM] * 13,
        out_specs=(ANY, ANY, VMEM, VMEM, ANY),
        scratch_shapes=[
            pltpu.VMEM((steps, area, pdim), BF),
            pltpu.VMEM(stem.shape, BF),
            pltpu.VMEM((4, TAPS, width, width), BF),
            pltpu.VMEM((width // 128, area, 128), F32),
            pltpu.VMEM(plain, BF),
            pltpu.VMEM(padded, BF),
            pltpu.VMEM(padded, BF),
            pltpu.VMEM((steps, 2 * LANE, width), F32),
            pltpu.VMEM((steps, 2 * LANE, width), F32),
            pltpu.VMEM((6, width, width), BF),
            pltpu.VMEM((3 * steps, heads), F32),
            pltpu.SMEM(counts.shape, jnp.int32),
            pltpu.SMEM(ends.shape, jnp.int32),
            pltpu.SMEM(rewards.shape, F32),
            pltpu.SMEM(ratios.shape, F32),
            pltpu.SMEM(valid.shape, jnp.int32),
            pltpu.VMEM(stored.shape, F32),
            pltpu.VMEM(head.shape, BF),
            pltpu.VMEM(discounts.shape, F32),
            pltpu.VMEM(lambdas.shape, F32),
            pltpu.SemaphoreType.DMA((32,)),
        ],
        compiler_params=pltpu.CompilerParams(vmem_limit_bytes=FRONT_GRANT),
        cost_estimate=pl.CostEstimate(flops=work, bytes_accessed=16 * 10**6, transcendentals=0),
    )(counts, ends, rewards, ratios, valid, frames.reshape(steps, area, pdim), stored, stem, first, second, head, discounts, lambdas)


def back(counts, middle, hidden, second, side):
    steps, width = middle.shape[0], middle.shape[-1]
    area = side * side
    return pl.pallas_call(
        functools.partial(back_kernel, side),
        out_shape=jax.ShapeDtypeStruct((steps, area, width), BF),
        in_specs=[HBM, ANY, ANY, HBM],
        out_specs=HBM,
        scratch_shapes=[
            pltpu.SMEM(counts.shape, jnp.int32),
            pltpu.VMEM(middle.shape, BF),
            pltpu.VMEM(hidden.shape, BF),
            pltpu.VMEM((TAPS, width, width), BF),
            pltpu.VMEM((6, width, width), BF),
            pltpu.VMEM((width // 128, area, 128), F32),
            pltpu.VMEM((steps, area, width), BF),
            pltpu.SemaphoreType.DMA((32,)),
        ],
        compiler_params=pltpu.CompilerParams(vmem_limit_bytes=BACK_GRANT),
        cost_estimate=pl.CostEstimate(
            flops=steps * area * 2 * width * TAPS * width, bytes_accessed=8 * 10**6, transcendentals=0
        ),
    )(counts, middle, hidden, second)


def target_kernel(steps, groups, chain_hbm, got_hbm, *refs):
    routed, targets_ref, load_ref = refs[:groups], refs[groups], refs[groups + 1]
    chain_ref, got_ref, sems = refs[groups + 2 : groups + 5]
    held = refs[groups + 5 :]
    group, shard = lax.axis_index("grp"), lax.axis_index("tm")
    shards, width = got_ref.shape[0], chain_ref.shape[1]
    pairs = ((got_hbm, got_ref), (chain_hbm.at[pl.ds(0, 3 * steps)], chain_ref)) + tuple(zip(routed, held))
    copies = [pltpu.make_async_copy(src, dst, sems.at[i]) for i, (src, dst) in enumerate(pairs)]
    for copy in copies:
        copy.start()
    for copy in copies:
        copy.wait()
    zero = jnp.zeros((1, width), F32)
    carry, first = zero, zero
    kept_carry, kept_first = zero, zero
    for s in range(shards - 1, -1, -1):
        carry = got_ref[s, 0:1] + got_ref[s, 1:2] * carry + got_ref[s, 2:3] * first
        first = got_ref[s, 3:4]
        follows = jnp.full((1, width), shard + 1, jnp.int32) == s
        kept_carry = jnp.where(follows, carry, kept_carry)
        kept_first = jnp.where(follows, first, kept_first)
    for t in range(steps):
        targets_ref[t : t + 1] = (
            chain_ref[t : t + 1]
            + chain_ref[steps + t : steps + t + 1] * kept_carry
            + chain_ref[2 * steps + t : 2 * steps + t + 1] * kept_first
        )
    load = jnp.int32(0)
    for codes in held:
        for t in range(steps):
            code = codes[0, t]
            load = load + jnp.where(code % groups == group, code // groups, 0)
    load_ref[0, 0] = load


def per_device(
    frames,
    sample_counts,
    dest_groups,
    episode_ends,
    valid_steps,
    rewards,
    ratios,
    stored_values,
    stem_weight,
    conv_first,
    conv_second,
    value_weight,
    discounts,
    lambdas,
):
    steps, side = frames.shape[1], frames.shape[2]
    width = stem_weight.shape[1]
    heads = value_weight.shape[1]
    groups, shards = lax.axis_size("grp"), lax.axis_size("tm")
    codes = sample_counts * groups + dest_groups
    routed = [codes]
    for far in range(1, groups):
        routed.append(lax.ppermute(codes, "grp", [(g, (g + far) % groups) for g in range(groups)]))
    middle, hidden, values, send, chain = front(
        sample_counts,
        episode_ends,
        rewards,
        ratios,
        valid_steps,
        frames[0],
        stored_values[0],
        stem_weight,
        conv_first,
        conv_second,
        value_weight,
        discounts[None],
        lambdas[None],
        shards,
    )
    got = lax.all_to_all(send, "tm", split_axis=0, concat_axis=0, tiled=True)
    latents = back(sample_counts, middle, hidden, conv_second, side)
    targets, load = pl.pallas_call(
        functools.partial(target_kernel, steps, groups),
        out_shape=(
            jax.ShapeDtypeStruct((steps, heads), F32),
            jax.ShapeDtypeStruct((1, 1), jnp.int32),
        ),
        in_specs=[ANY] * (2 + groups),
        out_specs=(VMEM, SMEM),
        scratch_shapes=[
            pltpu.VMEM((3 * steps, heads), F32),
            pltpu.VMEM(got.shape, F32),
            pltpu.SemaphoreType.DMA((2 + groups,)),
        ]
        + [pltpu.SMEM(codes.shape, jnp.int32)] * groups,
        compiler_params=pltpu.CompilerParams(vmem_limit_bytes=LAST_GRANT),
    )(chain, got, *routed)
    latents = latents.reshape(1, steps, side, side, width)
    return latents, values[None], targets[None], load


def solution(mesh):
    rows = P("grp", "tm")
    deep = P("grp", "tm", None)
    whole = P("grp", "tm", None, None, None)
    in_specs = (whole,) + (rows,) * 6 + (deep,) + (P(),) * 6
    out_specs = (whole, deep, deep, rows)
    return jax.shard_map(
        per_device, mesh=mesh, in_specs=in_specs, out_specs=out_specs, check_vma=False
    )
```

```python
import functools

import jax
import jax.numpy as jnp
from jax import lax
from jax.experimental import pallas as pl
from jax.experimental.pallas import tpu as pltpu
from jax.sharding import PartitionSpec as P

BF = jnp.bfloat16
F32 = jnp.float32
LANE = 8
TAPS = 9
WINO = True
CHUNK = 12
FRONT_GRANT = 60 * 2**20
BACK_GRANT = 60 * 2**20
LAST_GRANT = 40 * 2**20
TALL = 2**16


def tile_order(flat_ref, side):
    half, third = side // 2, side // LANE
    tiles = []
    for y in range(half):
        for j in range(third):
            for h in range(2):
                start = side * (half * h + y) + j
                rows = pl.ds(start, LANE, stride=third)
                parts = [flat_ref[c, rows, :] for c in range(flat_ref.shape[0])]
                tiles.append(jnp.concatenate(parts, axis=1))
    return jnp.stack(tiles).reshape(half, third, 2, LANE, -1)


def put_padded(out_ref, b, tiles, y0, half):
    count, third, _, _, width = tiles.shape
    place = lax.broadcasted_iota(jnp.int32, (count * 2, LANE, width), 1)
    before = pltpu.roll(tiles[:, third - 1].reshape(count * 2, LANE, width), 1, 1)
    before = jnp.where(place == 0, 0.0, before).reshape(count, 1, 2, LANE, width)
    after = pltpu.roll(tiles[:, 0].reshape(count * 2, LANE, width), LANE - 1, 1)
    after = jnp.where(place == LANE - 1, 0.0, after).reshape(count, 1, 2, LANE, width)
    wide = jnp.concatenate([before, tiles, after], axis=1)
    rows = wide.reshape(count, third + 2, 2 * LANE, width).astype(BF)
    out_ref[b, y0 + 1 : y0 + count + 1] = rows
    none = jnp.zeros((third + 2, 1, LANE, width), F32)
    if y0 + count == half:
        top = jnp.concatenate([none, wide[count - 1, :, 0:1]], axis=1)
        out_ref[b, 0] = top.reshape(third + 2, 2 * LANE, width).astype(BF)
    if y0 == 0:
        bottom = jnp.concatenate([wide[0, :, 1:2], none], axis=1)
        out_ref[b, half + 1] = bottom.reshape(third + 2, 2 * LANE, width).astype(BF)


def normed(hidden):
    wide = hidden.astype(F32)
    scale = lax.rsqrt(jnp.mean(wide * wide, axis=-1, keepdims=True) + 1e-05)
    return jnp.maximum(wide * scale, 0.0)


def conv(src_ref, b, weight_ref, mixed_ref, y0, count):
    _, tall, broad, rows, width = src_ref.shape
    third = broad - 2
    if not WINO:
        total = None
        for tap in range(TAPS):
            dy, dx = tap // 3, tap % 3
            window = src_ref[b, y0 + dy : y0 + dy + count, dx : dx + third].reshape(count * third * rows, width)
            part = jnp.dot(window, weight_ref[tap], preferred_element_type=F32)
            total = part if total is None else total + part
        return total.reshape(count, third, 2, LANE, weight_ref.shape[2])
    pairs = count // 2
    block = src_ref[b, y0 : y0 + count + 2].reshape(pairs + 1, 2, broad, rows, width)
    e0, e1, e2, e3 = block[:pairs, 0], block[:pairs, 1], block[1:, 0], block[1:, 1]
    parts = []
    for k, mix in enumerate((e0 - e2, e1 + e2, e2 - e1, e1 - e3)):
        total = None
        for dx in range(3):
            weight = (weight_ref[dx], mixed_ref[dx], mixed_ref[3 + dx], weight_ref[6 + dx])[k]
            window = mix[:, dx : dx + third].reshape(pairs * third * rows, width)
            part = jnp.dot(window, weight, preferred_element_type=F32)
            total = part if total is None else total + part
        parts.append(total)
    low = parts[0] + parts[1] + parts[2]
    high = parts[1] - parts[2] - parts[3]
    out = jnp.stack([x.reshape(pairs, third, 2, LANE, -1) for x in (low, high)], axis=1)
    return out.reshape(count, third, 2, LANE, -1)


def mix_weights(weight_ref, mixed_ref):
    if not WINO:
        return
    size = weight_ref.shape[1]

    def some(i, _):
        rows = pl.ds(pl.multiple_of(i * 64, 64), 64)
        for dx in range(3):
            outer = weight_ref[dx, rows].astype(F32) + weight_ref[6 + dx, rows].astype(F32)
            inner = weight_ref[3 + dx, rows].astype(F32)
            mixed_ref[dx, rows] = (0.5 * (outer + inner)).astype(BF)
            mixed_ref[3 + dx, rows] = (0.5 * (outer - inner)).astype(BF)
        return 0

    lax.fori_loop(0, size // 64, some, 0)


def window_rows(side):
    half, third = side // 2, side // LANE
    shape = (2 * LANE, side * side)
    tap = lax.broadcasted_iota(jnp.int32, shape, 0)
    at = lax.broadcasted_iota(jnp.int32, shape, 1)
    s = at % LANE
    h = (at // LANE) % 2
    j = (at // (2 * LANE)) % third
    y = at // (2 * LANE * third) + half * h
    x = s * third + j
    dy, dx = tap // 3 - 1, tap % 3 - 1
    out = ((dy == -1) & (y == side - 1)) | ((dy == 1) & (y == 0))
    out = out | ((dx == -1) & (x == side - 1)) | ((dx == 1) & (x == 0))
    inside = (tap == TAPS) | ((tap < TAPS) & jnp.logical_not(out))
    return jnp.where(inside, 1.0, 0.0).astype(BF)


def front_kernel(
    side,
    counts_hbm,
    ends_hbm,
    rewards_hbm,
    ratios_hbm,
    valid_hbm,
    frames_hbm,
    stored_hbm,
    stem_hbm,
    first_hbm,
    second_hbm,
    head_hbm,
    discounts_hbm,
    lambdas_hbm,
    middle_hbm,
    hidden_hbm,
    values_ref,
    send_ref,
    chain_hbm,
    frames,
    stem,
    weights,
    flat,
    hidden,
    act,
    mid,
    sums,
    kept,
    mixed,
    chain_ref,
    counts_ref,
    ends_ref,
    rewards_ref,
    ratios_ref,
    valid_ref,
    stored_ref,
    head_ref,
    discounts_ref,
    lambdas_ref,
    sems,
):
    steps = frames.shape[0]
    half = side // 2
    sem = iter(range(64))

    def load(src, dst):
        copy = pltpu.make_async_copy(src, dst, sems.at[next(sem)])
        copy.start()
        return copy

    stem_copy = load(stem_hbm, stem)
    frame_copies = [pltpu.make_async_copy(frames_hbm.at[b], frames.at[b], sems.at[next(sem)]) for b in range(steps)]
    weight_copies = [
        pltpu.make_async_copy(src, weights.at[i], sems.at[next(sem)])
        for i, src in enumerate((first_hbm.at[0], second_hbm.at[0], first_hbm.at[1], second_hbm.at[1]))
    ]
    frame_copies[0].start()
    weight_copies[0].start()
    frame_copies[1].start()
    small = [
        load(src, dst)
        for src, dst in (
            (counts_hbm, counts_ref),
            (ends_hbm, ends_ref),
            (rewards_hbm, rewards_ref),
            (ratios_hbm, ratios_ref),
            (valid_hbm, valid_ref),
            (stored_hbm, stored_ref),
            (head_hbm, head_ref),
            (discounts_hbm, discounts_ref),
            (lambdas_hbm, lambdas_ref),
        )
    ]
    hidden_copy = pltpu.make_async_copy(hidden, hidden_hbm, sems.at[next(sem)])
    middle_sem = 24

    def middle_copy(b):
        return pltpu.make_async_copy(mid.at[b], middle_hbm.at[b], sems.at[middle_sem + b])

    stem_copy.wait()

    def begin(b):
        for c in range(steps):

            @pl.when(b == c)
            def _():
                frame_copies[c].wait()
                if c + 2 < steps:
                    frame_copies[c + 2].start()
                else:
                    for i in range(c - 1, 2 * c - 2):
                        weight_copies[i].start()

        rows = jnp.maximum(jnp.dot(frames[b], stem[...], preferred_element_type=F32), 0.0)
        for c in range(flat.shape[0]):
            flat[c] = rows[:, 128 * c : 128 * c + 128]
        start = tile_order(flat, side).astype(BF)
        hidden[b] = start.reshape(hidden.shape[1:])
        put_padded(act, b, normed(start), 0, half)

    def layer(l, _):
        def first(b, _):
            @pl.when(l == 0)
            def _():
                begin(b)

            @pl.when((l == 0) & (b == 0))
            def _():
                weight_copies[0].wait()
                mix_weights(weights.at[0], mixed)

            @pl.when((l == 1) & (b == 0))
            def _():
                weight_copies[2].wait()
                mix_weights(weights.at[2], mixed)

            for y0 in range(0, half, CHUNK):
                out = conv(act, b, weights.at[2 * l], mixed, y0, CHUNK)
                put_padded(mid, b, jnp.maximum(out, 0.0), y0, half)

            @pl.when(l == 1)
            def _():
                middle_copy(b).start()

            return 0

        def second(b, _):
            for y0 in range(0, half, CHUNK):
                out = conv(mid, b, weights.at[1], mixed, y0, CHUNK)
                now = hidden[b, y0 : y0 + CHUNK].astype(F32).reshape(out.shape) + out
                now = now.astype(BF)
                hidden[b, y0 : y0 + CHUNK] = now.reshape((CHUNK,) + hidden.shape[2:])
                put_padded(act, b, normed(now), y0, half)
            return 0

        lax.fori_loop(0, steps, first, 0)

        @pl.when(l == 0)
        def _():
            weight_copies[1].wait()
            mix_weights(weights.at[1], mixed)
            lax.fori_loop(0, steps, second, 0, unroll=2)
            hidden_copy.start()

        return 0

    lax.fori_loop(0, 2, layer, 0)

    select = window_rows(side)
    width = hidden.shape[-1]

    def total(b, _):
        block = mid[b, 1 : half + 1, 1 : mid.shape[2] - 1].reshape(side * side, width)
        rows = hidden[b].reshape(side * side, width)
        sums[b] = jnp.dot(select, block, preferred_element_type=F32)
        kept[b] = jnp.dot(select, rows, preferred_element_type=F32)
        return 0

    lax.fori_loop(0, steps, total, 0)
    weight_copies[3].wait()
    pooled = None
    for tap in range(TAPS):
        exact = jnp.concatenate([sums[b, tap : tap + 1] for b in range(steps)], axis=0)
        parts, rest = [], exact
        for _ in range(3):
            part = rest.astype(BF)
            parts.append(part.astype(F32))
            rest = rest - part.astype(F32)
        stacked = jnp.concatenate(parts + [jnp.zeros_like(exact)], axis=0).astype(BF)
        term = jnp.dot(stacked, weights[3, tap], preferred_element_type=F32)
        pooled = term if pooled is None else pooled + term
    pooled = pooled[0:steps] + pooled[steps : 2 * steps] + pooled[2 * steps : 3 * steps]
    pooled = (pooled + jnp.concatenate([kept[b, TAPS : TAPS + 1] for b in range(steps)], axis=0)) * (1.0 / (side * side))
    for copy in small:
        copy.wait()
    fresh = jnp.dot(
        pooled,
        head_ref[...].astype(F32),
        precision=lax.Precision.HIGHEST,
        preferred_element_type=F32,
    )
    discount = discounts_ref[...]
    trace = lambdas_ref[...]
    rows = []
    for t in range(steps):
        live = jnp.full((1, fresh.shape[1]), counts_ref[0, t], jnp.int32) > 0
        rows.append(jnp.where(live, fresh[t : t + 1], stored_ref[t : t + 1]))
        values_ref[t : t + 1] = rows[t]
    add = jnp.zeros_like(discount)
    mul = jnp.ones_like(discount)
    last = jnp.zeros_like(discount)
    for t in range(steps - 1, -1, -1):
        going = 1.0 - ends_ref[0, t].astype(F32)
        cut = jnp.minimum(1.0, ratios_ref[0, t])
        weight = discount * going * (1.0 - trace * cut)
        step_mul = discount * trace * cut * going
        reward = rewards_ref[0, t]
        if t == steps - 1:
            add = reward + step_mul * add
            last = weight
        else:
            add = reward + weight * rows[t + 1] + step_mul * add
            last = step_mul * last
        mul = step_mul * mul
        valid = valid_ref[0, t].astype(F32)
        chain_ref[t : t + 1] = valid * add
        chain_ref[steps + t : steps + t + 1] = valid * mul
        chain_ref[2 * steps + t : 2 * steps + t + 1] = valid * last
    chain_copy = load(chain_ref, chain_hbm.at[pl.ds(0, 3 * steps)])
    shards = send_ref.shape[0]
    for place, row in enumerate((add, mul, last, rows[0])):
        send_ref[:, place : place + 1, :] = jnp.broadcast_to(row[None], (shards, 1, row.shape[1]))
    chain_copy.wait()
    hidden_copy.wait()
    for b in range(steps):
        middle_copy(b).wait()


def back_kernel(
    side, counts_hbm, middle_hbm, hidden_hbm, second_hbm, out_hbm, counts_ref, mid, hidden, weight, mixed, flat, done, sems
):
    steps = mid.shape[0]
    counts_copy = pltpu.make_async_copy(counts_hbm, counts_ref, sems.at[16])
    counts_copy.start()
    half, third = side // 2, side // LANE
    copies = []

    def load(i, src, dst):
        copy = pltpu.make_async_copy(src, dst, sems.at[i])
        copy.start()
        return copy

    weight_copy = load(0, second_hbm.at[1], weight)
    for b in range(steps):
        copies.append(
            (
                load(1 + 3 * b, middle_hbm.at[b], mid.at[b]),
                load(2 + 3 * b, hidden_hbm.at[b], hidden.at[b]),
            )
        )
    counts_copy.wait()
    weight_copy.wait()
    mix_weights(weight, mixed)

    def finish(b, _):
        pltpu.make_async_copy(middle_hbm.at[b], mid.at[b], sems.at[1 + 3 * b]).wait()
        pltpu.make_async_copy(hidden_hbm.at[b], hidden.at[b], sems.at[2 + 3 * b]).wait()
        live = counts_ref[0, b] > 0
        for y0 in range(0, half, CHUNK):
            out = conv(mid, b, weight, mixed, y0, CHUNK)
            out = hidden[b, y0 : y0 + CHUNK].astype(F32).reshape(out.shape) + out
            out = jnp.where(live, out, jnp.zeros_like(out))
            for y in range(CHUNK):
                for j in range(third):
                    for h in range(2):
                        start = side * (half * h + y0 + y) + j
                        for c in range(flat.shape[0]):
                            flat[c, pl.ds(start, LANE, stride=third), :] = out[y, j, h, :, 128 * c : 128 * c + 128]
        for c in range(flat.shape[0]):
            done[b, :, 128 * c : 128 * c + 128] = flat[c].astype(BF)
        pltpu.make_async_copy(done.at[b], out_hbm.at[b], sems.at[3 + 3 * b]).start()
        return 0

    lax.fori_loop(0, steps, finish, 0)
    for b in range(steps):
        pltpu.make_async_copy(done.at[b], out_hbm.at[b], sems.at[3 + 3 * b]).wait()


SMEM = pl.BlockSpec(memory_space=pltpu.SMEM)
VMEM = pl.BlockSpec(memory_space=pltpu.VMEM)
ANY = pl.BlockSpec(memory_space=pl.ANY)
HBM = pl.BlockSpec(memory_space=pltpu.HBM)


def front(counts, ends, rewards, ratios, valid, frames, stored, stem, first, second, head, discounts, lambdas, shards):
    steps, side, _, pdim = frames.shape
    width, heads = stem.shape[1], head.shape[1]
    half, third = side // 2, side // LANE
    padded = (steps, half + 2, third + 2, 2 * LANE, width)
    plain = (steps, half, third, 2 * LANE, width)
    area = side * side
    work = steps * area * 2 * width * (pdim + 3 * TAPS * width)
    return pl.pallas_call(
        functools.partial(front_kernel, side),
        out_shape=(
            jax.ShapeDtypeStruct(padded, BF),
            jax.ShapeDtypeStruct(plain, BF),
            jax.ShapeDtypeStruct((steps, heads), F32),
            jax.ShapeDtypeStruct((shards, 4, heads), F32),
            jax.ShapeDtypeStruct((TALL, heads), F32),
        ),
        in_specs=[HBM] * 13,
        out_specs=(ANY, ANY, VMEM, VMEM, ANY),
        scratch_shapes=[
            pltpu.VMEM((steps, area, pdim), BF),
            pltpu.VMEM(stem.shape, BF),
            pltpu.VMEM((4, TAPS, width, width), BF),
            pltpu.VMEM((width // 128, area, 128), F32),
            pltpu.VMEM(plain, BF),
            pltpu.VMEM(padded, BF),
            pltpu.VMEM(padded, BF),
            pltpu.VMEM((steps, 2 * LANE, width), F32),
            pltpu.VMEM((steps, 2 * LANE, width), F32),
            pltpu.VMEM((6, width, width), BF),
            pltpu.VMEM((3 * steps, heads), F32),
            pltpu.SMEM(counts.shape, jnp.int32),
            pltpu.SMEM(ends.shape, jnp.int32),
            pltpu.SMEM(rewards.shape, F32),
            pltpu.SMEM(ratios.shape, F32),
            pltpu.SMEM(valid.shape, jnp.int32),
            pltpu.VMEM(stored.shape, F32),
            pltpu.VMEM(head.shape, BF),
            pltpu.VMEM(discounts.shape, F32),
            pltpu.VMEM(lambdas.shape, F32),
            pltpu.SemaphoreType.DMA((32,)),
        ],
        compiler_params=pltpu.CompilerParams(vmem_limit_bytes=FRONT_GRANT),
        cost_estimate=pl.CostEstimate(flops=work, bytes_accessed=16 * 10**6, transcendentals=0),
    )(counts, ends, rewards, ratios, valid, frames.reshape(steps, area, pdim), stored, stem, first, second, head, discounts, lambdas)


def back(counts, middle, hidden, second, side):
    steps, width = middle.shape[0], middle.shape[-1]
    area = side * side
    return pl.pallas_call(
        functools.partial(back_kernel, side),
        out_shape=jax.ShapeDtypeStruct((steps, area, width), BF),
        in_specs=[HBM, ANY, ANY, HBM],
        out_specs=HBM,
        scratch_shapes=[
            pltpu.SMEM(counts.shape, jnp.int32),
            pltpu.VMEM(middle.shape, BF),
            pltpu.VMEM(hidden.shape, BF),
            pltpu.VMEM((TAPS, width, width), BF),
            pltpu.VMEM((6, width, width), BF),
            pltpu.VMEM((width // 128, area, 128), F32),
            pltpu.VMEM((steps, area, width), BF),
            pltpu.SemaphoreType.DMA((32,)),
        ],
        compiler_params=pltpu.CompilerParams(vmem_limit_bytes=BACK_GRANT),
        cost_estimate=pl.CostEstimate(
            flops=steps * area * 2 * width * TAPS * width, bytes_accessed=8 * 10**6, transcendentals=0
        ),
    )(counts, middle, hidden, second)


def target_kernel(steps, groups, chain_hbm, got_hbm, *refs):
    routed, targets_ref, load_ref = refs[:groups], refs[groups], refs[groups + 1]
    chain_ref, got_ref, sems = refs[groups + 2 : groups + 5]
    held = refs[groups + 5 :]
    group, shard = lax.axis_index("grp"), lax.axis_index("tm")
    shards, width = got_ref.shape[0], chain_ref.shape[1]
    pairs = ((got_hbm, got_ref), (chain_hbm.at[pl.ds(0, 3 * steps)], chain_ref)) + tuple(zip(routed, held))
    copies = [pltpu.make_async_copy(src, dst, sems.at[i]) for i, (src, dst) in enumerate(pairs)]
    for copy in copies:
        copy.start()
    for copy in copies:
        copy.wait()
    zero = jnp.zeros((1, width), F32)
    carry, first = zero, zero
    kept_carry, kept_first = zero, zero
    for s in range(shards - 1, -1, -1):
        carry = got_ref[s, 0:1] + got_ref[s, 1:2] * carry + got_ref[s, 2:3] * first
        first = got_ref[s, 3:4]
        follows = jnp.full((1, width), shard + 1, jnp.int32) == s
        kept_carry = jnp.where(follows, carry, kept_carry)
        kept_first = jnp.where(follows, first, kept_first)
    for t in range(steps):
        targets_ref[t : t + 1] = (
            chain_ref[t : t + 1]
            + chain_ref[steps + t : steps + t + 1] * kept_carry
            + chain_ref[2 * steps + t : 2 * steps + t + 1] * kept_first
        )
    load = jnp.int32(0)
    for codes in held:
        for t in range(steps):
            code = codes[0, t]
            load = load + jnp.where(code % groups == group, code // groups, 0)
    load_ref[0, 0] = load


def per_device(
    frames,
    sample_counts,
    dest_groups,
    episode_ends,
    valid_steps,
    rewards,
    ratios,
    stored_values,
    stem_weight,
    conv_first,
    conv_second,
    value_weight,
    discounts,
    lambdas,
):
    steps, side = frames.shape[1], frames.shape[2]
    width = stem_weight.shape[1]
    heads = value_weight.shape[1]
    groups, shards = lax.axis_size("grp"), lax.axis_size("tm")
    codes = sample_counts * groups + dest_groups
    routed = [codes]
    for far in range(groups - 1, 0, -1):
        routed.append(lax.ppermute(codes, "grp", [(g, (g + far) % groups) for g in range(groups)]))
    middle, hidden, values, send, chain = front(
        sample_counts,
        episode_ends,
        rewards,
        ratios,
        valid_steps,
        frames[0],
        stored_values[0],
        stem_weight,
        conv_first,
        conv_second,
        value_weight,
        discounts[None],
        lambdas[None],
        shards,
    )
    got = lax.all_to_all(send, "tm", split_axis=0, concat_axis=0, tiled=True)
    latents = back(sample_counts, middle, hidden, conv_second, side)
    targets, load = pl.pallas_call(
        functools.partial(target_kernel, steps, groups),
        out_shape=(
            jax.ShapeDtypeStruct((steps, heads), F32),
            jax.ShapeDtypeStruct((1, 1), jnp.int32),
        ),
        in_specs=[ANY] * (2 + groups),
        out_specs=(VMEM, SMEM),
        scratch_shapes=[
            pltpu.VMEM((3 * steps, heads), F32),
            pltpu.VMEM(got.shape, F32),
            pltpu.SemaphoreType.DMA((2 + groups,)),
        ]
        + [pltpu.SMEM(codes.shape, jnp.int32)] * groups,
        compiler_params=pltpu.CompilerParams(vmem_limit_bytes=LAST_GRANT),
    )(chain, got, *routed)
    latents = latents.reshape(1, steps, side, side, width)
    return latents, values[None], targets[None], load


def solution(mesh):
    rows = P("grp", "tm")
    deep = P("grp", "tm", None)
    whole = P("grp", "tm", None, None, None)
    in_specs = (whole,) + (rows,) * 6 + (deep,) + (P(),) * 6
    out_specs = (whole, deep, deep, rows)
    return jax.shard_map(
        per_device, mesh=mesh, in_specs=in_specs, out_specs=out_specs, check_vma=False
    )
```

```python
import functools

import jax
import jax.numpy as jnp
from jax import lax
from jax.experimental import pallas as pl
from jax.experimental.pallas import tpu as pltpu
from jax.sharding import PartitionSpec as P

BF = jnp.bfloat16
F32 = jnp.float32
LANE = 8
TAPS = 9
WINO = True
CHUNK = 12
FRONT_GRANT = 60 * 2**20
BACK_GRANT = 60 * 2**20
LAST_GRANT = 40 * 2**20
TALL = 2**16


def tile_order(flat_ref, side):
    half, third = side // 2, side // LANE
    tiles = []
    for y in range(half):
        for j in range(third):
            for h in range(2):
                start = side * (half * h + y) + j
                rows = pl.ds(start, LANE, stride=third)
                parts = [flat_ref[c, rows, :] for c in range(flat_ref.shape[0])]
                tiles.append(jnp.concatenate(parts, axis=1))
    return jnp.stack(tiles).reshape(half, third, 2, LANE, -1)


def put_padded(out_ref, b, tiles, y0, half):
    count, third, _, _, width = tiles.shape
    place = lax.broadcasted_iota(jnp.int32, (count * 2, LANE, width), 1)
    before = pltpu.roll(tiles[:, third - 1].reshape(count * 2, LANE, width), 1, 1)
    before = jnp.where(place == 0, 0.0, before).reshape(count, 1, 2, LANE, width)
    after = pltpu.roll(tiles[:, 0].reshape(count * 2, LANE, width), LANE - 1, 1)
    after = jnp.where(place == LANE - 1, 0.0, after).reshape(count, 1, 2, LANE, width)
    wide = jnp.concatenate([before, tiles, after], axis=1)
    rows = wide.reshape(count, third + 2, 2 * LANE, width).astype(BF)
    out_ref[b, y0 + 1 : y0 + count + 1] = rows
    none = jnp.zeros((third + 2, 1, LANE, width), F32)
    if y0 + count == half:
        top = jnp.concatenate([none, wide[count - 1, :, 0:1]], axis=1)
        out_ref[b, 0] = top.reshape(third + 2, 2 * LANE, width).astype(BF)
    if y0 == 0:
        bottom = jnp.concatenate([wide[0, :, 1:2], none], axis=1)
        out_ref[b, half + 1] = bottom.reshape(third + 2, 2 * LANE, width).astype(BF)


def normed(hidden):
    wide = hidden.astype(F32)
    scale = lax.rsqrt(jnp.mean(wide * wide, axis=-1, keepdims=True) + 1e-05)
    return jnp.maximum(wide * scale, 0.0)


def conv(src_ref, b, weight_ref, mixed_ref, y0, count):
    _, tall, broad, rows, width = src_ref.shape
    third = broad - 2
    if not WINO:
        total = None
        for tap in range(TAPS):
            dy, dx = tap // 3, tap % 3
            window = src_ref[b, y0 + dy : y0 + dy + count, dx : dx + third].reshape(count * third * rows, width)
            part = jnp.dot(window, weight_ref[tap], preferred_element_type=F32)
            total = part if total is None else total + part
        return total.reshape(count, third, 2, LANE, weight_ref.shape[2])
    pairs = count // 2
    block = src_ref[b, y0 : y0 + count + 2].reshape(pairs + 1, 2, broad, rows, width)
    e0, e1, e2, e3 = block[:pairs, 0], block[:pairs, 1], block[1:, 0], block[1:, 1]
    parts = []
    for k, mix in enumerate((e0 - e2, e1 + e2, e2 - e1, e1 - e3)):
        total = None
        for dx in range(3):
            weight = (weight_ref[dx], mixed_ref[dx], mixed_ref[3 + dx], weight_ref[6 + dx])[k]
            window = mix[:, dx : dx + third].reshape(pairs * third * rows, width)
            part = jnp.dot(window, weight, preferred_element_type=F32)
            total = part if total is None else total + part
        parts.append(total)
    low = parts[0] + parts[1] + parts[2]
    high = parts[1] - parts[2] - parts[3]
    out = jnp.stack([x.reshape(pairs, third, 2, LANE, -1) for x in (low, high)], axis=1)
    return out.reshape(count, third, 2, LANE, -1)


def mix_weights(weight_ref, mixed_ref):
    if not WINO:
        return
    size = weight_ref.shape[1]

    def some(i, _):
        rows = pl.ds(pl.multiple_of(i * 64, 64), 64)
        for dx in range(3):
            outer = weight_ref[dx, rows].astype(F32) + weight_ref[6 + dx, rows].astype(F32)
            inner = weight_ref[3 + dx, rows].astype(F32)
            mixed_ref[dx, rows] = (0.5 * (outer + inner)).astype(BF)
            mixed_ref[3 + dx, rows] = (0.5 * (outer - inner)).astype(BF)
        return 0

    lax.fori_loop(0, size // 64, some, 0)


def window_rows(side):
    half, third = side // 2, side // LANE
    shape = (2 * LANE, side * side)
    tap = lax.broadcasted_iota(jnp.int32, shape, 0)
    at = lax.broadcasted_iota(jnp.int32, shape, 1)
    s = at % LANE
    h = (at // LANE) % 2
    j = (at // (2 * LANE)) % third
    y = at // (2 * LANE * third) + half * h
    x = s * third + j
    dy, dx = tap // 3 - 1, tap % 3 - 1
    out = ((dy == -1) & (y == side - 1)) | ((dy == 1) & (y == 0))
    out = out | ((dx == -1) & (x == side - 1)) | ((dx == 1) & (x == 0))
    inside = (tap == TAPS) | ((tap < TAPS) & jnp.logical_not(out))
    return jnp.where(inside, 1.0, 0.0).astype(BF)


def front_kernel(
    side,
    counts_hbm,
    ends_hbm,
    rewards_hbm,
    ratios_hbm,
    valid_hbm,
    frames_hbm,
    stored_hbm,
    stem_hbm,
    first_hbm,
    second_hbm,
    head_hbm,
    discounts_hbm,
    lambdas_hbm,
    middle_hbm,
    hidden_hbm,
    values_ref,
    send_ref,
    chain_hbm,
    frames,
    stem,
    weights,
    flat,
    hidden,
    act,
    mid,
    sums,
    kept,
    mixed,
    chain_ref,
    counts_ref,
    ends_ref,
    rewards_ref,
    ratios_ref,
    valid_ref,
    stored_ref,
    head_ref,
    discounts_ref,
    lambdas_ref,
    sems,
):
    steps = frames.shape[0]
    half = side // 2
    sem = iter(range(64))

    def load(src, dst):
        copy = pltpu.make_async_copy(src, dst, sems.at[next(sem)])
        copy.start()
        return copy

    stem_copy = load(stem_hbm, stem)
    frame_copies = [pltpu.make_async_copy(frames_hbm.at[b], frames.at[b], sems.at[next(sem)]) for b in range(steps)]
    weight_copies = [
        pltpu.make_async_copy(src, weights.at[i], sems.at[next(sem)])
        for i, src in enumerate((first_hbm.at[0], second_hbm.at[0], first_hbm.at[1], second_hbm.at[1]))
    ]
    frame_copies[0].start()
    weight_copies[0].start()
    frame_copies[1].start()
    small = [
        load(src, dst)
        for src, dst in (
            (counts_hbm, counts_ref),
            (ends_hbm, ends_ref),
            (rewards_hbm, rewards_ref),
            (ratios_hbm, ratios_ref),
            (valid_hbm, valid_ref),
            (stored_hbm, stored_ref),
            (head_hbm, head_ref),
            (discounts_hbm, discounts_ref),
            (lambdas_hbm, lambdas_ref),
        )
    ]
    hidden_copy = pltpu.make_async_copy(hidden, hidden_hbm, sems.at[next(sem)])
    middle_sem = 24

    def middle_copy(b):
        return pltpu.make_async_copy(mid.at[b], middle_hbm.at[b], sems.at[middle_sem + b])

    stem_copy.wait()

    def begin(b):
        for c in range(steps):

            @pl.when(b == c)
            def _():
                frame_copies[c].wait()
                if c + 2 < steps:
                    frame_copies[c + 2].start()
                else:
                    for i in range(c - 1, 2 * c - 2):
                        weight_copies[i].start()

        rows = jnp.maximum(jnp.dot(frames[b], stem[...], preferred_element_type=F32), 0.0)
        for c in range(flat.shape[0]):
            flat[c] = rows[:, 128 * c : 128 * c + 128]
        start = tile_order(flat, side).astype(BF)
        hidden[b] = start.reshape(hidden.shape[1:])
        put_padded(act, b, normed(start), 0, half)

    def layer(l, _):
        def first(b, _):
            @pl.when(l == 0)
            def _():
                begin(b)

            @pl.when((l == 0) & (b == 0))
            def _():
                weight_copies[0].wait()
                mix_weights(weights.at[0], mixed)

            @pl.when((l == 1) & (b == 0))
            def _():
                weight_copies[2].wait()
                mix_weights(weights.at[2], mixed)

            for y0 in range(0, half, CHUNK):
                out = conv(act, b, weights.at[2 * l], mixed, y0, CHUNK)
                put_padded(mid, b, jnp.maximum(out, 0.0), y0, half)

            @pl.when(l == 1)
            def _():
                middle_copy(b).start()

            return 0

        def second(b, _):
            row = jnp.zeros((1, hidden.shape[-1]), F32)
            for y0 in range(0, half, CHUNK):
                out = conv(mid, b, weights.at[1], mixed, y0, CHUNK)
                now = hidden[b, y0 : y0 + CHUNK].astype(F32).reshape(out.shape) + out
                now = now.astype(BF)
                hidden[b, y0 : y0 + CHUNK] = now.reshape((CHUNK,) + hidden.shape[2:])
                sum_here = jnp.sum(now.astype(F32).reshape(-1, LANE, now.shape[-1]), axis=0)
                row = row + jnp.sum(sum_here, axis=0, keepdims=True)
                put_padded(act, b, normed(now), y0, half)
            kept[b, TAPS : TAPS + 1] = row
            return 0

        lax.fori_loop(0, steps, first, 0, unroll=2)

        @pl.when(l == 0)
        def _():
            weight_copies[1].wait()
            mix_weights(weights.at[1], mixed)
            lax.fori_loop(0, steps, second, 0, unroll=2)
            hidden_copy.start()

        return 0

    lax.fori_loop(0, 2, layer, 0)

    select = window_rows(side)
    width = hidden.shape[-1]

    def total(b, _):
        block = mid[b, 1 : half + 1, 1 : mid.shape[2] - 1].reshape(side * side, width)
        sums[b] = jnp.dot(select, block, preferred_element_type=F32)
        return 0

    lax.fori_loop(0, steps, total, 0)
    weight_copies[3].wait()
    pooled = None
    for tap in range(TAPS):
        exact = jnp.concatenate([sums[b, tap : tap + 1] for b in range(steps)], axis=0)
        parts, rest = [], exact
        for _ in range(3):
            part = rest.astype(BF)
            parts.append(part.astype(F32))
            rest = rest - part.astype(F32)
        stacked = jnp.concatenate(parts + [jnp.zeros_like(exact)], axis=0).astype(BF)
        term = jnp.dot(stacked, weights[3, tap], preferred_element_type=F32)
        pooled = term if pooled is None else pooled + term
    pooled = pooled[0:steps] + pooled[steps : 2 * steps] + pooled[2 * steps : 3 * steps]
    pooled = (pooled + jnp.concatenate([kept[b, TAPS : TAPS + 1] for b in range(steps)], axis=0)) * (1.0 / (side * side))
    for copy in small:
        copy.wait()
    fresh = jnp.dot(
        pooled,
        head_ref[...].astype(F32),
        precision=lax.Precision.HIGHEST,
        preferred_element_type=F32,
    )
    discount = discounts_ref[...]
    trace = lambdas_ref[...]
    rows = []
    for t in range(steps):
        live = jnp.full((1, fresh.shape[1]), counts_ref[0, t], jnp.int32) > 0
        rows.append(jnp.where(live, fresh[t : t + 1], stored_ref[t : t + 1]))
        values_ref[t : t + 1] = rows[t]
    add = jnp.zeros_like(discount)
    mul = jnp.ones_like(discount)
    last = jnp.zeros_like(discount)
    for t in range(steps - 1, -1, -1):
        going = 1.0 - ends_ref[0, t].astype(F32)
        cut = jnp.minimum(1.0, ratios_ref[0, t])
        weight = discount * going * (1.0 - trace * cut)
        step_mul = discount * trace * cut * going
        reward = rewards_ref[0, t]
        if t == steps - 1:
            add = reward + step_mul * add
            last = weight
        else:
            add = reward + weight * rows[t + 1] + step_mul * add
            last = step_mul * last
        mul = step_mul * mul
        valid = valid_ref[0, t].astype(F32)
        chain_ref[t : t + 1] = valid * add
        chain_ref[steps + t : steps + t + 1] = valid * mul
        chain_ref[2 * steps + t : 2 * steps + t + 1] = valid * last
    chain_copy = load(chain_ref, chain_hbm.at[pl.ds(0, 3 * steps)])
    shards = send_ref.shape[0]
    for place, row in enumerate((add, mul, last, rows[0])):
        send_ref[:, place : place + 1, :] = jnp.broadcast_to(row[None], (shards, 1, row.shape[1]))
    chain_copy.wait()
    hidden_copy.wait()
    for b in range(steps):
        middle_copy(b).wait()


def back_kernel(
    side, counts_hbm, middle_hbm, hidden_hbm, second_hbm, out_hbm, counts_ref, mid, hidden, weight, mixed, flat, done, sems
):
    steps = mid.shape[0]
    counts_copy = pltpu.make_async_copy(counts_hbm, counts_ref, sems.at[16])
    counts_copy.start()
    half, third = side // 2, side // LANE
    copies = []

    def load(i, src, dst):
        copy = pltpu.make_async_copy(src, dst, sems.at[i])
        copy.start()
        return copy

    weight_copy = load(0, second_hbm.at[1], weight)
    for b in range(steps):
        copies.append(
            (
                load(1 + 3 * b, middle_hbm.at[b], mid.at[b]),
                load(2 + 3 * b, hidden_hbm.at[b], hidden.at[b]),
            )
        )
    counts_copy.wait()
    weight_copy.wait()
    mix_weights(weight, mixed)

    def finish(b, _):
        pltpu.make_async_copy(middle_hbm.at[b], mid.at[b], sems.at[1 + 3 * b]).wait()
        pltpu.make_async_copy(hidden_hbm.at[b], hidden.at[b], sems.at[2 + 3 * b]).wait()
        live = counts_ref[0, b] > 0
        for y0 in range(0, half, CHUNK):
            out = conv(mid, b, weight, mixed, y0, CHUNK)
            out = hidden[b, y0 : y0 + CHUNK].astype(F32).reshape(out.shape) + out
            out = jnp.where(live, out, jnp.zeros_like(out))
            for y in range(CHUNK):
                for j in range(third):
                    for h in range(2):
                        start = side * (half * h + y0 + y) + j
                        for c in range(flat.shape[0]):
                            flat[c, pl.ds(start, LANE, stride=third), :] = out[y, j, h, :, 128 * c : 128 * c + 128]
        for c in range(flat.shape[0]):
            done[b, :, 128 * c : 128 * c + 128] = flat[c].astype(BF)
        pltpu.make_async_copy(done.at[b], out_hbm.at[b], sems.at[3 + 3 * b]).start()
        return 0

    lax.fori_loop(0, steps, finish, 0)
    for b in range(steps):
        pltpu.make_async_copy(done.at[b], out_hbm.at[b], sems.at[3 + 3 * b]).wait()


SMEM = pl.BlockSpec(memory_space=pltpu.SMEM)
VMEM = pl.BlockSpec(memory_space=pltpu.VMEM)
ANY = pl.BlockSpec(memory_space=pl.ANY)
HBM = pl.BlockSpec(memory_space=pltpu.HBM)


def front(counts, ends, rewards, ratios, valid, frames, stored, stem, first, second, head, discounts, lambdas, shards):
    steps, side, _, pdim = frames.shape
    width, heads = stem.shape[1], head.shape[1]
    half, third = side // 2, side // LANE
    padded = (steps, half + 2, third + 2, 2 * LANE, width)
    plain = (steps, half, third, 2 * LANE, width)
    area = side * side
    work = steps * area * 2 * width * (pdim + 3 * TAPS * width)
    return pl.pallas_call(
        functools.partial(front_kernel, side),
        out_shape=(
            jax.ShapeDtypeStruct(padded, BF),
            jax.ShapeDtypeStruct(plain, BF),
            jax.ShapeDtypeStruct((steps, heads), F32),
            jax.ShapeDtypeStruct((shards, 4, heads), F32),
            jax.ShapeDtypeStruct((TALL, heads), F32),
        ),
        in_specs=[HBM] * 13,
        out_specs=(ANY, ANY, VMEM, VMEM, ANY),
        scratch_shapes=[
            pltpu.VMEM((steps, area, pdim), BF),
            pltpu.VMEM(stem.shape, BF),
            pltpu.VMEM((4, TAPS, width, width), BF),
            pltpu.VMEM((width // 128, area, 128), F32),
            pltpu.VMEM(plain, BF),
            pltpu.VMEM(padded, BF),
            pltpu.VMEM(padded, BF),
            pltpu.VMEM((steps, 2 * LANE, width), F32),
            pltpu.VMEM((steps, 2 * LANE, width), F32),
            pltpu.VMEM((6, width, width), BF),
            pltpu.VMEM((3 * steps, heads), F32),
            pltpu.SMEM(counts.shape, jnp.int32),
            pltpu.SMEM(ends.shape, jnp.int32),
            pltpu.SMEM(rewards.shape, F32),
            pltpu.SMEM(ratios.shape, F32),
            pltpu.SMEM(valid.shape, jnp.int32),
            pltpu.VMEM(stored.shape, F32),
            pltpu.VMEM(head.shape, BF),
            pltpu.VMEM(discounts.shape, F32),
            pltpu.VMEM(lambdas.shape, F32),
            pltpu.SemaphoreType.DMA((32,)),
        ],
        compiler_params=pltpu.CompilerParams(vmem_limit_bytes=FRONT_GRANT),
        cost_estimate=pl.CostEstimate(flops=work, bytes_accessed=16 * 10**6, transcendentals=0),
    )(counts, ends, rewards, ratios, valid, frames.reshape(steps, area, pdim), stored, stem, first, second, head, discounts, lambdas)


def back(counts, middle, hidden, second, side):
    steps, width = middle.shape[0], middle.shape[-1]
    area = side * side
    return pl.pallas_call(
        functools.partial(back_kernel, side),
        out_shape=jax.ShapeDtypeStruct((steps, area, width), BF),
        in_specs=[HBM, ANY, ANY, HBM],
        out_specs=HBM,
        scratch_shapes=[
            pltpu.SMEM(counts.shape, jnp.int32),
            pltpu.VMEM(middle.shape, BF),
            pltpu.VMEM(hidden.shape, BF),
            pltpu.VMEM((TAPS, width, width), BF),
            pltpu.VMEM((6, width, width), BF),
            pltpu.VMEM((width // 128, area, 128), F32),
            pltpu.VMEM((steps, area, width), BF),
            pltpu.SemaphoreType.DMA((32,)),
        ],
        compiler_params=pltpu.CompilerParams(vmem_limit_bytes=BACK_GRANT),
        cost_estimate=pl.CostEstimate(
            flops=steps * area * 2 * width * TAPS * width, bytes_accessed=8 * 10**6, transcendentals=0
        ),
    )(counts, middle, hidden, second)


def target_kernel(steps, groups, chain_hbm, got_hbm, *refs):
    routed, targets_ref, load_ref = refs[:groups], refs[groups], refs[groups + 1]
    chain_ref, got_ref, sems = refs[groups + 2 : groups + 5]
    held = refs[groups + 5 :]
    group, shard = lax.axis_index("grp"), lax.axis_index("tm")
    shards, width = got_ref.shape[0], chain_ref.shape[1]
    pairs = ((got_hbm, got_ref), (chain_hbm.at[pl.ds(0, 3 * steps)], chain_ref)) + tuple(zip(routed, held))
    copies = [pltpu.make_async_copy(src, dst, sems.at[i]) for i, (src, dst) in enumerate(pairs)]
    for copy in copies:
        copy.start()
    for copy in copies:
        copy.wait()
    zero = jnp.zeros((1, width), F32)
    carry, first = zero, zero
    kept_carry, kept_first = zero, zero
    for s in range(shards - 1, -1, -1):
        carry = got_ref[s, 0:1] + got_ref[s, 1:2] * carry + got_ref[s, 2:3] * first
        first = got_ref[s, 3:4]
        follows = jnp.full((1, width), shard + 1, jnp.int32) == s
        kept_carry = jnp.where(follows, carry, kept_carry)
        kept_first = jnp.where(follows, first, kept_first)
    for t in range(steps):
        targets_ref[t : t + 1] = (
            chain_ref[t : t + 1]
            + chain_ref[steps + t : steps + t + 1] * kept_carry
            + chain_ref[2 * steps + t : 2 * steps + t + 1] * kept_first
        )
    load = jnp.int32(0)
    for codes in held:
        for t in range(steps):
            code = codes[0, t]
            load = load + jnp.where(code % groups == group, code // groups, 0)
    load_ref[0, 0] = load


def per_device(
    frames,
    sample_counts,
    dest_groups,
    episode_ends,
    valid_steps,
    rewards,
    ratios,
    stored_values,
    stem_weight,
    conv_first,
    conv_second,
    value_weight,
    discounts,
    lambdas,
):
    steps, side = frames.shape[1], frames.shape[2]
    width = stem_weight.shape[1]
    heads = value_weight.shape[1]
    groups, shards = lax.axis_size("grp"), lax.axis_size("tm")
    codes = sample_counts * groups + dest_groups
    routed = [codes]
    for far in range(groups - 1, 0, -1):
        routed.append(lax.ppermute(codes, "grp", [(g, (g + far) % groups) for g in range(groups)]))
    middle, hidden, values, send, chain = front(
        sample_counts,
        episode_ends,
        rewards,
        ratios,
        valid_steps,
        frames[0],
        stored_values[0],
        stem_weight,
        conv_first,
        conv_second,
        value_weight,
        discounts[None],
        lambdas[None],
        shards,
    )
    got = lax.all_to_all(send, "tm", split_axis=0, concat_axis=0, tiled=True)
    latents = back(sample_counts, middle, hidden, conv_second, side)
    targets, load = pl.pallas_call(
        functools.partial(target_kernel, steps, groups),
        out_shape=(
            jax.ShapeDtypeStruct((steps, heads), F32),
            jax.ShapeDtypeStruct((1, 1), jnp.int32),
        ),
        in_specs=[ANY] * (2 + groups),
        out_specs=(VMEM, SMEM),
        scratch_shapes=[
            pltpu.VMEM((3 * steps, heads), F32),
            pltpu.VMEM(got.shape, F32),
            pltpu.SemaphoreType.DMA((2 + groups,)),
        ]
        + [pltpu.SMEM(codes.shape, jnp.int32)] * groups,
        compiler_params=pltpu.CompilerParams(vmem_limit_bytes=LAST_GRANT),
    )(chain, got, *routed)
    latents = latents.reshape(1, steps, side, side, width)
    return latents, values[None], targets[None], load


def solution(mesh):
    rows = P("grp", "tm")
    deep = P("grp", "tm", None)
    whole = P("grp", "tm", None, None, None)
    in_specs = (whole,) + (rows,) * 6 + (deep,) + (P(),) * 6
    out_specs = (whole, deep, deep, rows)
    return jax.shard_map(
        per_device, mesh=mesh, in_specs=in_specs, out_specs=out_specs, check_vma=False
    )
```
